128 devices in a mesh: rep: 8 (over y, z_lo), tp: 16 (over x, z_hi, core).
Axes of the slice: x: 4, y: 4, z: 4 (z_hi: 2, z_lo: 2; z = z_hi * 2 + z_lo), core: 2. Of those that a mesh axis runs over, the one named last changes fastest.
Arguments:
- token_hidden_rows: bfloat16 [4, 512, 8192], P(None, 'rep', 'tp'), may hold values from -5400 to 5400
- input_norm_gain: float32 [8192], replicated, may hold values from 0.1 to 1.9
- frozen_query: bfloat16 [8192, 8192], P(('rep', 'tp')), may hold values from -20 to 20
- frozen_key_value: bfloat16 [8192, 2048], P(('rep', 'tp')), may hold values from -20 to 20
- frozen_output: bfloat16 [8192, 8192], P(('rep', 'tp')), may hold values from -20 to 20
- query_down_factor: bfloat16 [8192, 32], P(('rep', 'tp')), may hold values from -0.0625 to 0.0625
- query_up_factor: bfloat16 [32, 8192], replicated, may hold values from -12 to 12
- key_value_down_factor: bfloat16 [8192, 32], P(('rep', 'tp')), may hold values from -0.0625 to 0.0625
- key_value_up_factor: bfloat16 [32, 2048], replicated, may hold values from -12 to 12
- output_down_factor: bfloat16 [8192, 32], P(('rep', 'tp')), may hold values from -0.0625 to 0.0625
- output_up_factor: bfloat16 [32, 8192], replicated, may hold values from -12 to 12
- query_column_scale: float32 [8192], replicated, may hold values from 1 to 4
- key_value_column_scale: float32 [2048], replicated, may hold values from 2 to 8
- output_column_scale: float32 [8192], replicated, may hold values from 2 to 8
- cached_key_rows: bfloat16 [512, 8, 1024, 128], P(('rep', 'tp')), may hold values from -1900 to 1900
- cached_value_rows: bfloat16 [512, 8, 1024, 128], P(('rep', 'tp')), may hold values from -6 to 6
- lengths: int32 [512], P(('rep', 'tp')), may hold values from 1 to 1024, as said below
Outputs:
- output: bfloat16 [4, 512, 8192], P(None, 'rep', 'tp')
The draws below stay inside these ranges and needn't reach their ends.
Inputs may be any that keep to these rules, and one draw needn't show every extreme that they name: The first lengths[b] cache positions of sequence b are valid; in every draw some sequence holds all 1024.
All inputs are finite; a program needn't handle non-finite values.
Results may differ from the reference program's by a relative error of at most 0.0055.
The reference program's roundings to bfloat16 on the way count: a program that leaves them out, or rounds other values in their place, can miss the bound.
Values may be sent and summed in bfloat16 or wider, within the bound.
No kernel may reach another device: no remote copies, remote signals or barrier semaphores. Data moves between devices by JAX's collectives and lax.ppermute only.
A program may use at most 128 MiB of HBM per device.

```python
import math
import jax
import jax.numpy as jnp
from jax import lax

MODEL_WIDTH = 8192
QUERY_HEADS_COUNT = 64
KEY_VALUE_HEADS = 8
HEAD_SIZE = 128
ADAPTER_RANK = 32
DECODE_STEPS = 4
CACHE_SLOTS = 1024
QUERY_COLUMNS = 8192
KEY_VALUE_COLS = 2048
SEQUENCE_TOTAL = 512


def make_scales(key, row_count, col_count, top):
    row_key, col_key = jax.random.split(key)
    ramp_rows = 3.0 ** (jnp.arange(row_count, dtype=jnp.float32) / (row_count - 1))
    ramp_cols = 3.0 ** (jnp.arange(col_count, dtype=jnp.float32) / (col_count - 1))
    row_part = ramp_rows * jnp.exp(jax.random.uniform(row_key, (row_count,)) * math.log(top))
    col_part = ramp_cols * jnp.exp(jax.random.uniform(col_key, (col_count,)) * math.log(top))
    return row_part[:, None] * col_part[None, :]


def normal_entries(entry_random_key, scale_key, row_count, col_count, top):
    entries = jnp.clip(jax.random.normal(entry_random_key, (row_count, col_count)), -6.0, 6.0)
    return entries * make_scales(scale_key, row_count, col_count, top)


def draw_token_hidden_rows(key, part):
    key = jax.random.fold_in(key, 7)
    entry_random_key, scale_key = jax.random.split(key)
    value_rows = normal_entries(entry_random_key, scale_key, DECODE_STEPS * SEQUENCE_TOTAL, MODEL_WIDTH, 10.0)
    return value_rows.reshape(DECODE_STEPS, SEQUENCE_TOTAL, MODEL_WIDTH).astype(jnp.bfloat16)


def draw_frozen_query(key, part):
    key = jax.random.fold_in(key, 11)
    entry_random_key, scale_key = jax.random.split(key)
    value_rows = normal_entries(entry_random_key, scale_key, MODEL_WIDTH, QUERY_COLUMNS, 10.0)
    return jnp.clip(value_rows / math.sqrt(MODEL_WIDTH), -20.0, 20.0).astype(jnp.bfloat16)


def draw_frozen_key_value(key, part):
    key = jax.random.fold_in(key, 13)
    entry_random_key, scale_key = jax.random.split(key)
    value_rows = normal_entries(entry_random_key, scale_key, MODEL_WIDTH, KEY_VALUE_COLS, 10.0)
    return jnp.clip(value_rows / math.sqrt(MODEL_WIDTH), -20.0, 20.0).astype(jnp.bfloat16)


def draw_frozen_output(key, part):
    key = jax.random.fold_in(key, 17)
    entry_random_key, scale_key = jax.random.split(key)
    value_rows = normal_entries(entry_random_key, scale_key, QUERY_COLUMNS, MODEL_WIDTH, 10.0)
    return jnp.clip(value_rows / math.sqrt(QUERY_COLUMNS), -20.0, 20.0).astype(jnp.bfloat16)


def draw_cached_key_rows(key, part):
    key = jax.random.fold_in(key, 19)
    entry_random_key = jax.random.fold_in(key, 0)
    value_rows = jnp.clip(jax.random.normal(entry_random_key, (SEQUENCE_TOTAL, KEY_VALUE_HEADS, CACHE_SLOTS, HEAD_SIZE)), -6.0, 6.0)
    return value_rows.astype(jnp.bfloat16)


def draw_lengths(key, part):
    key = jax.random.fold_in(key, 23)
    length_key, pick_key = jax.random.split(key)
    drawn = jax.random.randint(length_key, (SEQUENCE_TOTAL,), 1, CACHE_SLOTS + 1)
    chosen = jax.random.randint(pick_key, (), 0, SEQUENCE_TOTAL)
    drawn = jnp.where(jnp.arange(SEQUENCE_TOTAL, dtype=jnp.int32) == chosen, CACHE_SLOTS, drawn)
    return drawn.astype(jnp.int32)


def shard_levels(rng, extent, shards, least, largest):
    def one(dim, shards_of):
        heights = jax.random.uniform(jax.random.fold_in(jax.random.fold_in(rng, 6), dim), (shards_of,), jnp.float32, least / len(shards), largest / len(shards))
        return jnp.repeat(jnp.exp(heights), extent[dim] // shards_of).reshape((-1,) + (1,) * (len(extent) - dim - 1))

    factor_of = one(*shards[0])
    for cut in shards[1:]:
        factor_of = factor_of * one(*cut)
    return factor_of


def gaussian(own_key, extent, deviation, most, pieces=(), kind=jnp.bfloat16):
    values = deviation * jax.random.normal(own_key, extent, jnp.float32)
    if pieces:
        values = values * shard_levels(own_key, extent, pieces, -0.22, 0.18)
    return jnp.clip(values, -most, most).astype(kind)


def setup_inputs(seed: int = 0) -> dict:
    key_list = jax.random.split(jax.random.key(seed), 18)
    token_hidden_rows = draw_token_hidden_rows(jax.random.fold_in(key_list[17], 71), 0)
    input_norm_gain = jnp.clip(1.0 + 0.18 * jax.random.normal(key_list[1], (MODEL_WIDTH,), jnp.float32), 0.1, 1.9)
    frozen_query = draw_frozen_query(jax.random.fold_in(key_list[17], 71), 0)
    frozen_key_value = draw_frozen_key_value(jax.random.fold_in(key_list[17], 71), 0)
    frozen_output = draw_frozen_output(jax.random.fold_in(key_list[17], 71), 0)
    query_down_factor = gaussian(key_list[5], (MODEL_WIDTH, ADAPTER_RANK), MODEL_WIDTH ** -0.5, 0.0625, ((0, 128),))
    query_up_factor = gaussian(key_list[6], (ADAPTER_RANK, QUERY_COLUMNS), 2.0, 12.0)
    key_value_down_factor = gaussian(key_list[7], (MODEL_WIDTH, ADAPTER_RANK), MODEL_WIDTH ** -0.5, 0.0625, ((0, 128),))
    key_value_up_factor = gaussian(key_list[8], (ADAPTER_RANK, KEY_VALUE_COLS), 2.0, 12.0)
    output_down_factor = gaussian(key_list[9], (QUERY_COLUMNS, ADAPTER_RANK), QUERY_COLUMNS ** -0.5, 0.0625, ((0, 128),))
    output_up_factor = gaussian(key_list[10], (ADAPTER_RANK, MODEL_WIDTH), 2.0, 12.0)
    query_column_scale = jnp.clip(jnp.exp(jax.random.uniform(key_list[11], (QUERY_COLUMNS,), jnp.float32, math.log(1.0), math.log(4.0))), 1.0, 4.0)
    key_value_column_scale = jnp.clip(jnp.exp(jax.random.uniform(key_list[12], (KEY_VALUE_COLS,), jnp.float32, math.log(2.0), math.log(8.0))), 2.0, 8.0)
    output_column_scale = jnp.clip(jnp.exp(jax.random.uniform(key_list[13], (MODEL_WIDTH,), jnp.float32, math.log(2.0), math.log(8.0))), 2.0, 8.0)
    cached_key_rows = draw_cached_key_rows(jax.random.fold_in(key_list[17], 71), 0)
    cached_value_rows = gaussian(key_list[15], (SEQUENCE_TOTAL, KEY_VALUE_HEADS, CACHE_SLOTS, HEAD_SIZE), 1.0, 6.0, ((0, 128),))
    lengths = draw_lengths(jax.random.fold_in(key_list[17], 71), 0)
    return dict(token_hidden_rows=token_hidden_rows, input_norm_gain=input_norm_gain, frozen_query=frozen_query, frozen_key_value=frozen_key_value, frozen_output=frozen_output, query_down_factor=query_down_factor, query_up_factor=query_up_factor, key_value_down_factor=key_value_down_factor, key_value_up_factor=key_value_up_factor, output_down_factor=output_down_factor, output_up_factor=output_up_factor, query_column_scale=query_column_scale, key_value_column_scale=key_value_column_scale, output_column_scale=output_column_scale, cached_key_rows=cached_key_rows, cached_value_rows=cached_value_rows, lengths=lengths)


EPSILON = 1e-06
NEG_LARGE = -1e+30

def merge_with_scale(base_weight, adapter_down_factor, adapter_up_factor, column_magnitude):
    merged_weight = base_weight.astype(jnp.float32) + jnp.dot(adapter_down_factor, adapter_up_factor, preferred_element_type=jnp.float32)
    col_norm = jnp.sqrt(lax.optimization_barrier(jnp.sum(merged_weight * merged_weight, axis=0)))
    return (merged_weight * (column_magnitude / col_norm)).astype(jnp.bfloat16)

def reference(token_hidden_rows, input_norm_gain, frozen_query, frozen_key_value, frozen_output, query_down_factor, query_up_factor, key_value_down_factor, key_value_up_factor, output_down_factor, output_up_factor, query_column_scale, key_value_column_scale, output_column_scale, cached_key_rows, cached_value_rows, lengths):
    query_weight = merge_with_scale(frozen_query, query_down_factor, query_up_factor, query_column_scale)
    key_value_weight = merge_with_scale(frozen_key_value, key_value_down_factor, key_value_up_factor, key_value_column_scale)
    output_weight = merge_with_scale(frozen_output, output_down_factor, output_up_factor, output_column_scale)
    features = token_hidden_rows.astype(jnp.float32)
    mean_sq = lax.optimization_barrier(jnp.mean(features * features, axis=-1, keepdims=True))
    normed = (features * lax.rsqrt(mean_sq + EPSILON) * input_norm_gain).astype(jnp.bfloat16)
    flat = normed.reshape(DECODE_STEPS * SEQUENCE_TOTAL, MODEL_WIDTH)
    tensor_group_width = QUERY_HEADS_COUNT // KEY_VALUE_HEADS
    query_every_head = jnp.dot(flat, query_weight, preferred_element_type=jnp.float32).astype(jnp.bfloat16)
    query_every_head = query_every_head.reshape(DECODE_STEPS, SEQUENCE_TOTAL, KEY_VALUE_HEADS, tensor_group_width, HEAD_SIZE)
    fresh_token_rows = jnp.dot(flat, key_value_weight, preferred_element_type=jnp.float32).astype(jnp.bfloat16)
    fresh_token_rows = fresh_token_rows.reshape(DECODE_STEPS, SEQUENCE_TOTAL, KEY_VALUE_HEADS, 2, HEAD_SIZE)
    inv_root = 1.0 / math.sqrt(HEAD_SIZE)
    order_ok = jnp.arange(DECODE_STEPS, dtype=jnp.int32)[None, :] <= jnp.arange(DECODE_STEPS, dtype=jnp.int32)[:, None]
    order_ok = order_ok[:, None, None, :]

    def one_sequence(items):
        query_seq, fresh_seq, keys_seq, values_seq, length = items
        query_f = query_seq.astype(jnp.float32)
        live_mask = jnp.arange(CACHE_SLOTS, dtype=jnp.int32) < length
        cache_scores = jnp.einsum('tghd,gjd->tghj', query_f, keys_seq.astype(jnp.float32)) * inv_root
        cache_scores = jnp.where(live_mask, cache_scores, NEG_LARGE)
        fresh_scores = jnp.einsum('tghd,ugd->tghu', query_f, fresh_seq[:, :, 0].astype(jnp.float32)) * inv_root
        fresh_scores = jnp.where(order_ok, fresh_scores, NEG_LARGE)
        peak_score = jnp.maximum(lax.optimization_barrier(jnp.max(cache_scores, axis=-1)), lax.optimization_barrier(jnp.max(fresh_scores, axis=-1)))
        cache_probs = jnp.where(live_mask, jnp.exp(cache_scores - peak_score[..., None]), 0.0)
        fresh_probs = jnp.where(order_ok, jnp.exp(fresh_scores - peak_score[..., None]), 0.0)
        weight_total = lax.optimization_barrier(jnp.sum(cache_probs, axis=-1)) + lax.optimization_barrier(jnp.sum(fresh_probs, axis=-1))
        cache_round = lax.optimization_barrier(cache_probs.astype(jnp.bfloat16)).astype(jnp.float32)
        fresh_round = lax.optimization_barrier(fresh_probs.astype(jnp.bfloat16)).astype(jnp.float32)
        context = jnp.einsum('tghj,gjd->tghd', cache_round, values_seq.astype(jnp.float32))
        context = context + jnp.einsum('tghu,ugd->tghd', fresh_round, fresh_seq[:, :, 1].astype(jnp.float32))
        return (context / weight_total[..., None]).astype(jnp.bfloat16)
    attended = lax.map(one_sequence, (jnp.transpose(query_every_head, (1, 0, 2, 3, 4)), jnp.transpose(fresh_token_rows, (1, 0, 2, 3, 4)), cached_key_rows, cached_value_rows, lengths))
    attended = jnp.transpose(attended, (1, 0, 2, 3, 4)).reshape(DECODE_STEPS * SEQUENCE_TOTAL, QUERY_COLUMNS)
    output = jnp.dot(attended, output_weight, preferred_element_type=jnp.float32).astype(jnp.bfloat16)
    return output.reshape(DECODE_STEPS, SEQUENCE_TOTAL, MODEL_WIDTH)
```

```python
import math

import jax
import jax.numpy as jnp
from jax import lax
from jax.experimental import pallas as pl
from jax.experimental.pallas import tpu as pltpu
from jax.sharding import PartitionSpec as P

EPSILON = 1e-06
NEG_LARGE = -1e30
AXES = ("rep", "tp")


def device_index(y, zl, x, zh, c):
    return (y * 2 + zl) * 16 + x * 4 + zh * 2 + c


def permute(value, target):
    pairs = []
    for y in range(4):
        for zl in range(2):
            for x in range(4):
                for zh in range(2):
                    for c in range(2):
                        pairs.append(
                            (device_index(y, zl, x, zh, c), device_index(*target(y, zl, x, zh, c)))
                        )
    return lax.ppermute(value, AXES, pairs)


def swap_low(value):
    return permute(value, lambda y, zl, x, zh, c: (y, 1 - zl, x, zh, c))


def swap_core(value):
    return permute(value, lambda y, zl, x, zh, c: (y, zl, x, zh, 1 - c))


def from_y(value, step):
    return permute(value, lambda y, zl, x, zh, c: ((y - step) % 4, zl, x, zh, c))


def from_x(value, step):
    return permute(value, lambda y, zl, x, zh, c: (y, zl, (x - step) % 4, zh, c))


def after(value, earlier):
    return lax.optimization_barrier((value, earlier))[0]


def pick(value, index, axis=0):
    return lax.dynamic_index_in_dim(value, index, axis, keepdims=False)


def share_sums(sums):
    spread = jnp.broadcast_to(sums[None, :], (8, sums.shape[0]))
    return jnp.sum(lax.all_to_all(spread, "rep", 0, 0, tiled=True), axis=0)


def pack_columns_kernel(place, query, key_value, down_q, down_kv, down_o, out):
    f32 = jnp.float32
    down_q, down_kv, down_o = (d[...].astype(f32) for d in (down_q, down_kv, down_o))
    blank = jnp.zeros_like(down_o)
    down = jnp.where(
        place[0] < 8,
        jnp.concatenate([down_q, down_kv, down_o, blank], axis=0),
        jnp.concatenate([down_o, blank, down_q, down_kv], axis=0),
    )
    down = down.T.astype(jnp.bfloat16)
    for i in range(4):
        for k in range(4):
            out[i, k] = query[:, (i * 4 + k) * 128 : (i * 4 + k + 1) * 128]
        out[i, 4] = key_value[:, i * 128 : (i + 1) * 128]
        out[i, 5] = down


def pack_columns(place, query, key_value, *downs):
    down = pl.BlockSpec((32, 64), lambda i, place: (0, 0))
    return pl.pallas_call(
        pack_columns_kernel,
        grid_spec=pltpu.PrefetchScalarGridSpec(
            num_scalar_prefetch=1,
            grid=(4,),
            in_specs=[
                pl.BlockSpec((64, 2048), lambda i, place: (0, i)),
                pl.BlockSpec((64, 512), lambda i, place: (0, i)),
                down,
                down,
                down,
            ],
            out_specs=pl.BlockSpec((4, 6, 64, 128), lambda i, place: (i, 0, 0, 0)),
        ),
        out_shape=jax.ShapeDtypeStruct((16, 6, 64, 128), jnp.bfloat16),
        cost_estimate=pl.CostEstimate(flops=0, bytes_accessed=2**22, transcendentals=0),
    )(place, query, key_value, *downs)


def unpack_columns_kernel(received, ups, block_a, block_b, down, out):
    lanes = lax.broadcasted_iota(jnp.int32, (64, 128), 1)
    for i in range(8):
        rows = slice(i * 64, (i + 1) * 64)
        first, second = received[i, 5], received[8 + i, 5]
        down[rows] = first
        down[512 + i * 64 : 512 + (i + 1) * 64] = second
        block_a[0, rows] = jnp.where(
            lanes < 64, first.astype(jnp.float32), second.astype(jnp.float32)
        ).astype(jnp.bfloat16)
        for k in range(5):
            block_a[1 + k, rows] = received[i, k]
            block_b[k, rows] = received[8 + i, k]
    for half in range(2):
        merged = jnp.dot(block_a[0], ups[half], preferred_element_type=jnp.float32)
        sums = []
        for k in range(5):
            rows = block_a[1 + k] if half == 0 else block_b[k]
            tile = merged[:, k * 128 : (k + 1) * 128] + rows.astype(jnp.float32)
            sums.append(jnp.sum(tile * tile, axis=0, keepdims=True))
        sums = jnp.concatenate(sums, axis=1)
        if half == 0:
            out[...] = sums
        else:
            out[...] += sums


def unpack_columns(received, ups):
    return pl.pallas_call(
        unpack_columns_kernel,
        out_shape=[
            jax.ShapeDtypeStruct((6, 512, 128), jnp.bfloat16),
            jax.ShapeDtypeStruct((5, 512, 128), jnp.bfloat16),
            jax.ShapeDtypeStruct((1024, 128), jnp.bfloat16),
            jax.ShapeDtypeStruct((1, 640), jnp.float32),
        ],
        compiler_params=pltpu.CompilerParams(vmem_limit_bytes=24 * 2**20),
        cost_estimate=pl.CostEstimate(flops=2**28, bytes_accessed=2**22, transcendentals=0),
    )(received, ups)


def multiply_slab_kernel(place, near, far, inverse, gain, ups, factor, block_a, block_b, *rest):
    out = rest[-1]
    value = None
    for half in range(2):
        tokens = jnp.where(place[2] == half, near[0], far[0]).astype(jnp.float32)
        normed = (tokens * inverse[...] * gain[0, half]).astype(jnp.bfloat16)
        merged = jnp.dot(block_a[0], ups[half], preferred_element_type=jnp.float32)
        tiles = []
        for k in range(5):
            rows = block_a[1 + k] if half == 0 else block_b[k]
            tiles.append(merged[:, k * 128 : (k + 1) * 128] + rows.astype(jnp.float32))
        weight = (jnp.concatenate(tiles, axis=1) * factor[...]).astype(jnp.bfloat16)
        part = jnp.dot(normed, weight, preferred_element_type=jnp.float32)
        value = part if value is None else value + part
    if len(rest) == 2:
        value = value + rest[0][...]
    out[...] = value


def multiply_slab(place, near, far, inverse, gains, blocks, ups, factor, total):
    def whole(shape):
        return pl.BlockSpec(shape, lambda i, place: (0,) * len(shape))

    operands = [near, far, inverse, gains, ups, factor, *blocks]
    specs = [
        pl.BlockSpec((1, 512, 512), lambda i, place: (place[0], 0, 0)),
        pl.BlockSpec((1, 512, 512), lambda i, place: (place[0], 0, 0)),
        whole((512, 1)),
        pl.BlockSpec((1, 2, 1, 512), lambda i, place: (place[1], 0, 0, 0)),
        whole((2, 128, 640)),
        whole((1, 640)),
    ]
    specs += [whole(block.shape) for block in blocks]
    if total is not None:
        operands.append(total)
        specs.append(whole((512, 640)))
    return pl.pallas_call(
        multiply_slab_kernel,
        grid_spec=pltpu.PrefetchScalarGridSpec(
            num_scalar_prefetch=1,
            grid=(1,),
            in_specs=specs,
            out_specs=whole((512, 640)),
        ),
        out_shape=jax.ShapeDtypeStruct((512, 640), jnp.float32),
        compiler_params=pltpu.CompilerParams(vmem_limit_bytes=40 * 2**20),
        cost_estimate=pl.CostEstimate(flops=2**30, bytes_accessed=2**22, transcendentals=0),
    )(place, *operands)


def attend_kernel(place, lengths, every, keys, values, out):
    f32, bf16 = jnp.float32, jnp.bfloat16
    inv_root = 1.0 / math.sqrt(128)
    both = every[...].astype(f32)
    fresh_keys = every[0, :, 512:]
    fresh_values = every[1, :, 512:]
    contract_last = (((1,), (1,)), ((), ()))
    fresh_column = lax.broadcasted_iota(jnp.int32, (32, 16), 1)
    fresh_row = lax.broadcasted_iota(jnp.int32, (32, 16), 0)
    slots = lax.broadcasted_iota(jnp.int32, (32, 1024), 1)
    pieces = []
    for b in range(4):
        rows = slice(b * 4, b * 4 + 4)
        query = jnp.concatenate(
            [both[h // 4, rows, (h % 4) * 128 : (h % 4 + 1) * 128] for h in range(8)], axis=0
        ).astype(bf16)
        live = slots < lengths[b]
        scores = lax.dot_general(query, keys[b, 0], contract_last, preferred_element_type=f32)
        scores = jnp.where(live, scores * inv_root, NEG_LARGE)
        order = (fresh_column >= b * 4) & (fresh_column - b * 4 <= fresh_row % 4)
        fresh = lax.dot_general(query, fresh_keys, contract_last, preferred_element_type=f32)
        fresh = jnp.where(order, fresh * inv_root, NEG_LARGE)
        peak = jnp.maximum(
            jnp.max(scores, axis=1, keepdims=True), jnp.max(fresh, axis=1, keepdims=True)
        )
        probs = jnp.where(live, jnp.exp(scores - peak), 0.0)
        fresh_probs = jnp.where(order, jnp.exp(fresh - peak), 0.0)
        total = jnp.sum(probs, axis=1, keepdims=True) + jnp.sum(fresh_probs, axis=1, keepdims=True)
        context = jnp.dot(probs.astype(bf16), values[b, 0], preferred_element_type=f32)
        context += jnp.dot(fresh_probs.astype(bf16), fresh_values, preferred_element_type=f32)
        context = context / total
        pieces.append(jnp.concatenate([context[h * 4 : h * 4 + 4] for h in range(8)], axis=1))
    out[0] = jnp.concatenate(pieces, axis=0).astype(bf16)


def attend(place, lengths, every, cached_key_rows, cached_value_rows):
    def slab(g, place, lengths):
        return (((g + place[1]) % 2) * 4 + (g // 2 + 4 - place[0]) % 4, 0, 0)

    cache = pl.BlockSpec((4, 1, 1024, 128), lambda g, place, lengths: (0, g, 0, 0))
    return pl.pallas_call(
        attend_kernel,
        grid_spec=pltpu.PrefetchScalarGridSpec(
            num_scalar_prefetch=2,
            grid=(8,),
            in_specs=[
                pl.BlockSpec((2, 16, 640), lambda g, place, lengths: (g, 0, 0)),
                cache,
                cache,
            ],
            out_specs=pl.BlockSpec((1, 16, 1024), slab),
        ),
        out_shape=jax.ShapeDtypeStruct((8, 16, 1024), jnp.bfloat16),
        compiler_params=pltpu.CompilerParams(vmem_limit_bytes=56 * 2**20),
        cost_estimate=pl.CostEstimate(flops=2**29, bytes_accessed=2**24, transcendentals=2**20),
    )(place, lengths, every, cached_key_rows, cached_value_rows)


def output_kernel(place, near_a, near_b, far_a, far_b, rows_0, rows_1, rows_2, rows_3, mine, other):
    weights = (rows_0, rows_1, rows_2, rows_3)
    total = None
    for j in range(4):
        parts = []
        for first, second in ((near_a, near_b), (far_a, far_b)):
            if j < 2:
                parts.append(first[:, :, j].reshape(256, 1024))
            else:
                parts.extend(second[:, e, j - 2].reshape(64, 1024) for e in range(4))
        part = jnp.dot(
            jnp.concatenate(parts, axis=0), weights[j][...], preferred_element_type=jnp.float32
        )
        total = part if total is None else total + part
    for cr in range(2):
        for e in range(4):
            for dl in range(2):
                for dh in range(2):
                    start = cr * 256 + e * 64 + dl * 32 + dh * 16
                    target = ((place[0] + e) % 4) * 4 + (place[1] ^ dh) * 2 + (place[2] ^ cr)
                    rows = total[start : start + 16]
                    if dl == 0:
                        mine[target] = rows
                    else:
                        other[target] = rows.astype(jnp.bfloat16)


def multiply_output(place, pieces, rows_o):
    def whole(shape):
        return pl.BlockSpec(shape, lambda i, place: (0,) * len(shape))

    operands = [*pieces, *rows_o]
    return pl.pallas_call(
        output_kernel,
        grid_spec=pltpu.PrefetchScalarGridSpec(
            num_scalar_prefetch=1,
            grid=(1,),
            in_specs=[whole(operand.shape) for operand in operands],
            out_specs=[whole((16, 16, 512)), whole((16, 16, 512))],
        ),
        out_shape=[
            jax.ShapeDtypeStruct((16, 16, 512), jnp.float32),
            jax.ShapeDtypeStruct((16, 16, 512), jnp.bfloat16),
        ],
        compiler_params=pltpu.CompilerParams(vmem_limit_bytes=40 * 2**20),
        cost_estimate=pl.CostEstimate(flops=2**31, bytes_accessed=2**23, transcendentals=0),
    )(place, *operands)


def per_device(
    token_hidden_rows,
    input_norm_gain,
    frozen_query,
    frozen_key_value,
    frozen_output,
    query_down_factor,
    query_up_factor,
    key_value_down_factor,
    key_value_up_factor,
    output_down_factor,
    output_up_factor,
    query_column_scale,
    key_value_column_scale,
    output_column_scale,
    cached_key_rows,
    cached_value_rows,
    lengths,
):
    f32, bf16 = jnp.float32, jnp.bfloat16
    r, t = lax.axis_index("rep"), lax.axis_index("tp")
    y, zl = r // 2, r % 2
    x, zh, c = t // 4, (t // 2) % 2, t % 2

    local = token_hidden_rows.reshape(256, 512)
    pair = jnp.concatenate(
        [
            permute(local, lambda y, zl, x, zh, c, s=s: (y, zh, x, zl ^ s, c))
            for s in range(2)
        ]
    )

    frozen = pack_columns(
        t.astype(jnp.int32).reshape(1),
        frozen_query,
        frozen_key_value,
        query_down_factor.T,
        key_value_down_factor.T,
        output_down_factor.T,
    )
    received = lax.all_to_all(frozen, "tp", 0, 0, tiled=True)

    up_q = lax.dynamic_slice_in_dim(query_up_factor, t * 512, 512, 1)
    up_kv = lax.dynamic_slice_in_dim(key_value_up_factor, t * 128, 128, 1)
    up_o = lax.dynamic_slice_in_dim(output_up_factor, t * 512, 512, 1)
    up_qkv = jnp.concatenate(
        [
            jnp.concatenate([up_q, jnp.zeros((32, 128), bf16)], axis=1),
            jnp.concatenate([jnp.zeros((32, 512), bf16), up_kv], axis=1),
        ],
        axis=0,
    )
    blank = jnp.zeros((64, 640), bf16)
    ups = jnp.stack(
        [jnp.concatenate([up_qkv, blank], axis=0), jnp.concatenate([blank, up_qkv], axis=0)]
    )
    up_out_a = jnp.concatenate(
        [jnp.zeros((64, 512), bf16), up_o, jnp.zeros((32, 512), bf16)], axis=0
    )
    up_out_b = jnp.concatenate([up_o, jnp.zeros((96, 512), bf16)], axis=0)
    scale_qkv = jnp.concatenate(
        [
            lax.dynamic_slice_in_dim(query_column_scale, t * 512, 512, 0),
            lax.dynamic_slice_in_dim(key_value_column_scale, t * 128, 128, 0),
        ]
    )
    scale_out = lax.dynamic_slice_in_dim(output_column_scale, t * 512, 512, 0)

    received, ups, up_out_a, up_out_b, scale_qkv, scale_out = lax.optimization_barrier(
        (received, ups, up_out_a, up_out_b, scale_qkv, scale_out)
    )
    own_a, own_b, down_own, sums = unpack_columns(received, ups)
    sums = share_sums(sums.reshape(640))
    factor_qkv = (scale_qkv / jnp.sqrt(sums)).reshape(1, 640)

    own_a, own_b, pair = lax.optimization_barrier((own_a, own_b, pair, sums))[:3]
    next_a, next_b = from_y(own_a, 1), from_y(own_b, 1)
    last_b, last_a = from_y(own_b, 3), from_y(own_a, 3)
    tokens = [pair] + [from_x(pair, step) for step in (1, 2, 3)]
    tokens, next_a, next_b, last_a, last_b = lax.optimization_barrier(
        (tokens, next_a, next_b, last_a, last_b)
    )
    far_a, far_b = from_y(next_a, 1), from_y(last_b, 3)

    frozen_o = after(frozen_output, next_a)
    own_o = lax.all_to_all(
        frozen_o.reshape(64, 16, 512).transpose(1, 0, 2), "tp", 0, 0, tiled=True
    ).reshape(1024, 512)
    merged_o = own_o.astype(f32) + jnp.concatenate(
        [
            jnp.dot(down_own[:512], up_out_a, preferred_element_type=f32),
            jnp.dot(down_own[512:], up_out_b, preferred_element_type=f32),
        ]
    )
    sums_o = jnp.sum(merged_o * merged_o, axis=0)

    near = jnp.stack(tokens)
    far = swap_core(near)
    near_wide, far_wide = near.astype(f32), far.astype(f32)
    square_sum = jnp.sum(near_wide * near_wide + far_wide * far_wide, axis=(0, 2))
    square_sum = square_sum + swap_low(square_sum)
    inverse = lax.rsqrt(square_sum / 8192.0 + EPSILON).reshape(512, 1)
    gains = pick(input_norm_gain.reshape(4, 2, 2, 1, 512), zl, 1)

    def project(step, blocks, total):
        place = jnp.stack([(y + step - x) % 4, (y + step) % 4, c]).astype(jnp.int32)
        return multiply_slab(
            place, near, far, inverse, gains, blocks, ups, factor_qkv, total
        )

    total = project(0, (own_a, own_b), None)
    total = project(1, (next_a, next_b), total)
    total = project(3, (last_a, last_b), total)
    total, far_a, far_b = lax.optimization_barrier((total, far_a, far_b))
    total = project(2, (far_a, far_b), total)

    sums_o = share_sums(after(sums_o, total))
    weight_o = (merged_o * (scale_out / jnp.sqrt(sums_o))).astype(bf16)
    rows_o = [weight_o] + [from_y(weight_o, step) for step in (1, 2, 3)]

    total = total.reshape(2, 256, 640)
    mine = zh ^ zl
    projected = (pick(total, mine) + swap_low(pick(total, 1 - mine))).astype(bf16)

    projected = projected.reshape(4, 16, 4, 640).transpose(1, 2, 0, 3).reshape(16, 16, 640)
    every = lax.all_to_all(projected, "tp", 0, 0, tiled=True)
    place = jnp.stack([y, zl]).astype(jnp.int32)
    attended = attend(place, lengths, every, cached_key_rows, cached_value_rows)

    attended, rows_o = lax.optimization_barrier((attended, rows_o))
    slabs = attended.reshape(2, 4, 16, 1024)

    def along_z(own, other):
        def flip(value, dl, dh):
            return permute(value, lambda y, zl, x, zh, c: (y, zl ^ dl, x, zh ^ dh, c))

        return jnp.stack([own, flip(own, 0, 1), flip(other, 1, 0), flip(other, 1, 1)])

    def along_x(value):
        return jnp.stack([value] + [from_x(value, step) for step in (1, 2, 3)])

    first = along_z(slabs[0, :2], slabs[1, :2])
    second = along_x(slabs[:, 2:])
    first = along_x(first)
    second = along_z(second[:, 0], second[:, 1])
    place = jnp.stack([x, zh, c]).astype(jnp.int32)
    mine, other = multiply_output(
        place, (first, second, swap_core(first), swap_core(second)), rows_o
    )
    result = (mine + swap_low(other).astype(f32)).astype(bf16)
    return result.reshape(16, 4, 4, 512).transpose(2, 0, 1, 3).reshape(4, 64, 512)


def solution(mesh):
    return jax.shard_map(
        per_device,
        mesh=mesh,
        in_specs=(
            P(None, "rep", "tp"),
            P(),
            P(("rep", "tp"), None),
            P(("rep", "tp"), None),
            P(("rep", "tp"), None),
            P(("rep", "tp"), None),
            P(),
            P(("rep", "tp"), None),
            P(),
            P(("rep", "tp"), None),
            P(),
            P(),
            P(),
            P(),
            P(("rep", "tp"), None, None, None),
            P(("rep", "tp"), None, None, None),
            P(("rep", "tp")),
        ),
        out_specs=P(None, "rep", "tp"),
        check_vma=False,
    )
```

```python
import math

import jax
import jax.numpy as jnp
from jax import lax
from jax.experimental import pallas as pl
from jax.experimental.pallas import tpu as pltpu
from jax.sharding import PartitionSpec as P

EPSILON = 1e-06
NEG_LARGE = -1e30
AXES = ("rep", "tp")


def device_index(y, zl, x, zh, c):
    return (y * 2 + zl) * 16 + x * 4 + zh * 2 + c


def permute(value, target):
    pairs = []
    for y in range(4):
        for zl in range(2):
            for x in range(4):
                for zh in range(2):
                    for c in range(2):
                        pairs.append(
                            (device_index(y, zl, x, zh, c), device_index(*target(y, zl, x, zh, c)))
                        )
    return lax.ppermute(value, AXES, pairs)


def swap_low(value):
    return permute(value, lambda y, zl, x, zh, c: (y, 1 - zl, x, zh, c))


def swap_core(value):
    return permute(value, lambda y, zl, x, zh, c: (y, zl, x, zh, 1 - c))


def from_y(value, step):
    return permute(value, lambda y, zl, x, zh, c: ((y - step) % 4, zl, x, zh, c))


def from_x(value, step):
    return permute(value, lambda y, zl, x, zh, c: (y, zl, (x - step) % 4, zh, c))


def after(value, earlier):
    return lax.optimization_barrier((value, earlier))[0]


def pick(value, index, axis=0):
    return lax.dynamic_index_in_dim(value, index, axis, keepdims=False)


def share_sums(sums):
    spread = jnp.broadcast_to(sums[None, :], (8, sums.shape[0]))
    return jnp.sum(lax.all_to_all(spread, "rep", 0, 0, tiled=True), axis=0)


def pack_columns_kernel(place, query, key_value, output, down_q, down_kv, down_o, out):
    f32 = jnp.float32
    down_q, down_kv, down_o = (d[...].astype(f32) for d in (down_q, down_kv, down_o))
    blank = jnp.zeros_like(down_o)
    down = jnp.where(
        place[0] < 8,
        jnp.concatenate([down_q, down_kv, down_o, blank], axis=0),
        jnp.concatenate([down_o, blank, down_q, down_kv], axis=0),
    )
    down = down.T.astype(jnp.bfloat16)
    for i in range(4):
        for k in range(4):
            columns = slice((i * 4 + k) * 128, (i * 4 + k + 1) * 128)
            out[i, k] = query[:, columns]
            out[i, 6 + k] = output[:, columns]
        out[i, 4] = key_value[:, i * 128 : (i + 1) * 128]
        out[i, 5] = down


def pack_columns(place, query, key_value, output, *downs):
    down = pl.BlockSpec((32, 64), lambda i, place: (0, 0))
    return pl.pallas_call(
        pack_columns_kernel,
        grid_spec=pltpu.PrefetchScalarGridSpec(
            num_scalar_prefetch=1,
            grid=(4,),
            in_specs=[
                pl.BlockSpec((64, 2048), lambda i, place: (0, i)),
                pl.BlockSpec((64, 512), lambda i, place: (0, i)),
                pl.BlockSpec((64, 2048), lambda i, place: (0, i)),
                down,
                down,
                down,
            ],
            out_specs=pl.BlockSpec((4, 10, 64, 128), lambda i, place: (i, 0, 0, 0)),
        ),
        out_shape=jax.ShapeDtypeStruct((16, 10, 64, 128), jnp.bfloat16),
        cost_estimate=pl.CostEstimate(flops=0, bytes_accessed=2**22, transcendentals=0),
    )(place, query, key_value, output, *downs)


def unpack_columns_kernel(received, ups, ups_out, block_a, block_b, rows_out, down, out):
    lanes = lax.broadcasted_iota(jnp.int32, (64, 128), 1)
    for i in range(8):
        rows = slice(i * 64, (i + 1) * 64)
        first, second = received[i, 5], received[8 + i, 5]
        down[0, rows] = first
        down[1, rows] = second
        block_a[0, rows] = jnp.where(
            lanes < 64, first.astype(jnp.float32), second.astype(jnp.float32)
        ).astype(jnp.bfloat16)
        for k in range(5):
            block_a[1 + k, rows] = received[i, k]
            block_b[k, rows] = received[8 + i, k]
        for k in range(4):
            for half in range(2):
                rows_out[half, rows, k * 128 : (k + 1) * 128] = received[half * 8 + i, 6 + k]
    total = None
    for half in range(2):
        merged = jnp.dot(block_a[0], ups[half], preferred_element_type=jnp.float32)
        sums = []
        for k in range(5):
            rows = block_a[1 + k] if half == 0 else block_b[k]
            tile = merged[:, k * 128 : (k + 1) * 128] + rows.astype(jnp.float32)
            sums.append(jnp.sum(tile * tile, axis=0, keepdims=True))
        merged = jnp.dot(down[half], ups_out[half], preferred_element_type=jnp.float32)
        merged = merged + rows_out[half].astype(jnp.float32)
        sums.append(jnp.sum(merged * merged, axis=0, keepdims=True))
        sums = jnp.concatenate(sums, axis=1)
        total = sums if total is None else total + sums
    out[...] = total


def unpack_columns(received, ups, ups_out):
    return pl.pallas_call(
        unpack_columns_kernel,
        out_shape=[
            jax.ShapeDtypeStruct((6, 512, 128), jnp.bfloat16),
            jax.ShapeDtypeStruct((5, 512, 128), jnp.bfloat16),
            jax.ShapeDtypeStruct((2, 512, 512), jnp.bfloat16),
            jax.ShapeDtypeStruct((2, 512, 128), jnp.bfloat16),
            jax.ShapeDtypeStruct((1, 1152), jnp.float32),
        ],
        compiler_params=pltpu.CompilerParams(vmem_limit_bytes=24 * 2**20),
        cost_estimate=pl.CostEstimate(flops=2**28, bytes_accessed=2**22, transcendentals=0),
    )(received, ups, ups_out)


def scale_rows_kernel(rows, down, ups, factor, out_a, out_b):
    for half, out in enumerate((out_a, out_b)):
        merged = jnp.dot(down[half], ups[half], preferred_element_type=jnp.float32)
        merged = rows[half].astype(jnp.float32) + merged
        out[...] = (merged * factor[...]).astype(jnp.bfloat16)


def scale_rows(rows, down, ups, factor):
    return pl.pallas_call(
        scale_rows_kernel,
        out_shape=[jax.ShapeDtypeStruct((512, 512), jnp.bfloat16)] * 2,
        compiler_params=pltpu.CompilerParams(vmem_limit_bytes=56 * 2**20),
        cost_estimate=pl.CostEstimate(flops=2**20, bytes_accessed=2**12, transcendentals=0),
    )(rows, down, ups, factor)


def token_sums_kernel(near, out):
    total = None
    for e in range(4):
        wide = near[e].astype(jnp.float32)
        part = jnp.sum(wide * wide, axis=1, keepdims=True)
        total = part if total is None else total + part
    out[...] = total


def token_sums(near):
    return pl.pallas_call(
        token_sums_kernel,
        out_shape=jax.ShapeDtypeStruct((512, 1), jnp.float32),
        compiler_params=pltpu.CompilerParams(vmem_limit_bytes=56 * 2**20),
        cost_estimate=pl.CostEstimate(flops=2**20, bytes_accessed=2**12, transcendentals=0),
    )(near)


def multiply_slabs_kernel(place, *refs):
    count = (place.shape[0] - 2) // 2
    slabs, refs = refs[: 3 * count], refs[3 * count :]
    inverse, ups, factor = refs[:3]
    blocks, rest = refs[3 : 3 + 2 * count], refs[3 + 2 * count :]
    value = None
    for i in range(count):
        near, far, gain = slabs[3 * i : 3 * i + 3]
        block_a, block_b = blocks[2 * i : 2 * i + 2]
        for half in range(2):
            tokens = jnp.where(place[2 * count] == half, near[0], far[0]).astype(jnp.float32)
            normed = (tokens * inverse[...] * gain[0, half]).astype(jnp.bfloat16)
            merged = jnp.dot(block_a[0], ups[half], preferred_element_type=jnp.float32)
            tiles = []
            for k in range(5):
                rows = block_a[1 + k] if half == 0 else block_b[k]
                tiles.append(merged[:, k * 128 : (k + 1) * 128] + rows.astype(jnp.float32))
            weight = (jnp.concatenate(tiles, axis=1) * factor[...]).astype(jnp.bfloat16)
            part = jnp.dot(normed, weight, preferred_element_type=jnp.float32)
            value = part if value is None else value + part
    if len(rest) == 1:
        rest[0][...] = value
    else:
        value = value + rest[0][...]
        swapped = place[2 * count + 1] == 1
        rest[1][...] = jnp.where(swapped, value[:256], value[256:])
        rest[2][...] = jnp.where(swapped, value[256:], value[:256])


def multiply_slabs(place, near, far, inverse, gains, blocks, ups, factor, total):
    count = len(blocks) // 2

    def whole(shape):
        return pl.BlockSpec(shape, lambda i, place: (0,) * len(shape))

    operands, specs = [], []
    for k in range(count):
        operands += [near, far, gains]
        specs += [pl.BlockSpec((1, 512, 512), lambda i, place, k=k: (place[k], 0, 0))] * 2
        specs.append(
            pl.BlockSpec((1, 2, 1, 512), lambda i, place, k=k: (place[count + k], 0, 0, 0))
        )
    rest = [inverse, ups, factor, *blocks] + ([] if total is None else [total])
    operands += rest
    specs += [whole(operand.shape) for operand in rest]
    rows = 512 if total is None else 256
    shape = jax.ShapeDtypeStruct((rows, 640), jnp.float32)
    return pl.pallas_call(
        multiply_slabs_kernel,
        grid_spec=pltpu.PrefetchScalarGridSpec(
            num_scalar_prefetch=1,
            grid=(1,),
            in_specs=specs,
            out_specs=whole((rows, 640)) if total is None else [whole((rows, 640))] * 2,
        ),
        out_shape=shape if total is None else [shape] * 2,
        compiler_params=pltpu.CompilerParams(vmem_limit_bytes=56 * 2**20),
        cost_estimate=pl.CostEstimate(
            flops=2**20, bytes_accessed=2**12, transcendentals=0
        ),
    )(place, *operands)


def attend_kernel(place, lengths, every, keys, values, out):
    f32, bf16 = jnp.float32, jnp.bfloat16
    inv_root = 1.0 / math.sqrt(128)
    both = every[...].astype(f32)
    fresh_keys = every[0, :, 512:]
    fresh_values = every[1, :, 512:]
    contract_last = (((1,), (1,)), ((), ()))
    fresh_column = lax.broadcasted_iota(jnp.int32, (128, 16), 1)
    fresh_row = lax.broadcasted_iota(jnp.int32, (128, 16), 0)
    slots = lax.broadcasted_iota(jnp.int32, (32, 1024), 1)
    blank = jnp.zeros((32, 128), bf16)
    queries = [
        jnp.concatenate(
            [
                both[h // 4, b * 4 : b * 4 + 4, (h % 4) * 128 : (h % 4 + 1) * 128]
                for h in range(8)
            ],
            axis=0,
        ).astype(bf16)
        for b in range(4)
    ]
    fresh = lax.dot_general(
        jnp.concatenate(queries, axis=0), fresh_keys, contract_last, preferred_element_type=f32
    )
    own = (fresh_row // 32) * 4
    order = (fresh_column >= own) & (fresh_column - own <= fresh_row % 4)
    fresh = jnp.where(order, fresh * inv_root, NEG_LARGE)
    scores = []
    for b in (0, 2):
        query = jnp.concatenate(
            [
                jnp.concatenate([queries[b], blank], axis=1),
                jnp.concatenate([blank, queries[b + 1]], axis=1),
            ],
            axis=0,
        )
        key = jnp.concatenate([keys[b, 0], keys[b + 1, 0]], axis=1)
        scores.append(
            lax.dot_general(query, key, contract_last, preferred_element_type=f32)
        )
    live = jnp.concatenate([slots < lengths[b] for b in range(4)], axis=0)
    scores = jnp.where(live, jnp.concatenate(scores, axis=0) * inv_root, NEG_LARGE)
    peak = jnp.maximum(
        jnp.max(scores, axis=1, keepdims=True), jnp.max(fresh, axis=1, keepdims=True)
    )
    probs = jnp.where(live, jnp.exp(scores - peak), 0.0)
    fresh_probs = jnp.where(order, jnp.exp(fresh - peak), 0.0)
    total = jnp.sum(probs, axis=1, keepdims=True) + jnp.sum(fresh_probs, axis=1, keepdims=True)
    rounded = probs.astype(bf16)
    contexts = []
    for b in (0, 2):
        value = jnp.concatenate([values[b, 0], values[b + 1, 0]], axis=1)
        part = jnp.dot(rounded[b * 32 : b * 32 + 64], value, preferred_element_type=f32)
        contexts += [part[:32, :128], part[32:, 128:]]
    context = jnp.concatenate(contexts, axis=0)
    context += jnp.dot(fresh_probs.astype(bf16), fresh_values, preferred_element_type=f32)
    context = context / total
    pieces = [
        jnp.concatenate(
            [context[b * 32 + h * 4 : b * 32 + h * 4 + 4] for h in range(8)], axis=1
        )
        for b in range(4)
    ]
    out[0] = jnp.concatenate(pieces, axis=0).astype(bf16)


def attend(place, lengths, every, cached_key_rows, cached_value_rows):
    def slab(g, place, lengths):
        return (((g + place[1]) % 2) * 4 + (g // 2 + 4 - place[0]) % 4, 0, 0)

    cache = pl.BlockSpec((4, 1, 1024, 128), lambda g, place, lengths: (0, g, 0, 0))
    return pl.pallas_call(
        attend_kernel,
        grid_spec=pltpu.PrefetchScalarGridSpec(
            num_scalar_prefetch=2,
            grid=(8,),
            in_specs=[
                pl.BlockSpec((2, 16, 640), lambda g, place, lengths: (g, 0, 0)),
                cache,
                cache,
            ],
            out_specs=pl.BlockSpec((1, 16, 1024), slab),
        ),
        out_shape=jax.ShapeDtypeStruct((8, 16, 1024), jnp.bfloat16),
        compiler_params=pltpu.CompilerParams(vmem_limit_bytes=56 * 2**20),
        cost_estimate=pl.CostEstimate(flops=2**20, bytes_accessed=2**12, transcendentals=0),
    )(place, lengths, every, cached_key_rows, cached_value_rows)


def output_kernel(place, near_a, near_b, far_a, far_b, *refs):
    weights, (mine, other) = refs[:8], refs[8:]
    total = None
    for j in range(4):
        parts = []
        for first, second in ((near_a, near_b), (far_a, far_b)):
            if j < 2:
                parts.append(first[:, :, j].reshape(256, 1024))
            else:
                parts.extend(second[:, e, j - 2].reshape(64, 1024) for e in range(4))
        rows = jnp.concatenate(parts, axis=0)
        for half in range(2):
            part = jnp.dot(
                rows[:, half * 512 : (half + 1) * 512],
                weights[2 * j + half][...],
                preferred_element_type=jnp.float32,
            )
            total = part if total is None else total + part
    for cr in range(2):
        for e in range(4):
            for dl in range(2):
                for dh in range(2):
                    start = cr * 256 + e * 64 + dl * 32 + dh * 16
                    target = ((place[0] + e) % 4) * 4 + (place[1] ^ dh) * 2 + (place[2] ^ cr)
                    rows = total[start : start + 16]
                    if dl == 0:
                        mine[target] = rows
                    else:
                        other[target] = rows.astype(jnp.bfloat16)


def multiply_output(place, pieces, rows_o):
    def whole(shape):
        return pl.BlockSpec(shape, lambda i, place: (0,) * len(shape))

    operands = [*pieces, *rows_o]
    return pl.pallas_call(
        output_kernel,
        grid_spec=pltpu.PrefetchScalarGridSpec(
            num_scalar_prefetch=1,
            grid=(1,),
            in_specs=[whole(operand.shape) for operand in operands],
            out_specs=[whole((16, 16, 512)), whole((16, 16, 512))],
        ),
        out_shape=[
            jax.ShapeDtypeStruct((16, 16, 512), jnp.float32),
            jax.ShapeDtypeStruct((16, 16, 512), jnp.bfloat16),
        ],
        compiler_params=pltpu.CompilerParams(vmem_limit_bytes=40 * 2**20),
        cost_estimate=pl.CostEstimate(flops=2**31, bytes_accessed=2**23, transcendentals=0),
    )(place, *operands)


def per_device(
    token_hidden_rows,
    input_norm_gain,
    frozen_query,
    frozen_key_value,
    frozen_output,
    query_down_factor,
    query_up_factor,
    key_value_down_factor,
    key_value_up_factor,
    output_down_factor,
    output_up_factor,
    query_column_scale,
    key_value_column_scale,
    output_column_scale,
    cached_key_rows,
    cached_value_rows,
    lengths,
):
    f32, bf16 = jnp.float32, jnp.bfloat16
    r, t = lax.axis_index("rep"), lax.axis_index("tp")
    y, zl = r // 2, r % 2
    x, zh, c = t // 4, (t // 2) % 2, t % 2

    local = token_hidden_rows.transpose(1, 0, 2).reshape(256, 512)
    pair = jnp.concatenate(
        [
            permute(local, lambda y, zl, x, zh, c, s=s: (y, zh, x, zl ^ s, c))
            for s in range(2)
        ]
    )

    frozen = pack_columns(
        t.astype(jnp.int32).reshape(1),
        frozen_query,
        frozen_key_value,
        frozen_output,
        query_down_factor.T,
        key_value_down_factor.T,
        output_down_factor.T,
    )
    received = lax.all_to_all(frozen, "tp", 0, 0, tiled=True)

    up_q = lax.dynamic_slice_in_dim(query_up_factor, t * 512, 512, 1)
    up_kv = lax.dynamic_slice_in_dim(key_value_up_factor, t * 128, 128, 1)
    up_o = lax.dynamic_slice_in_dim(output_up_factor, t * 512, 512, 1)
    up_qkv = jnp.concatenate(
        [
            jnp.concatenate([up_q, jnp.zeros((32, 128), bf16)], axis=1),
            jnp.concatenate([jnp.zeros((32, 512), bf16), up_kv], axis=1),
        ],
        axis=0,
    )
    blank = jnp.zeros((64, 640), bf16)
    ups = jnp.stack(
        [jnp.concatenate([up_qkv, blank], axis=0), jnp.concatenate([blank, up_qkv], axis=0)]
    )
    blank = jnp.zeros((32, 512), bf16)
    ups_out = jnp.stack(
        [
            jnp.concatenate([blank, blank, up_o, blank]),
            jnp.concatenate([up_o, blank, blank, blank]),
        ]
    )
    scale_qkv = jnp.concatenate(
        [
            lax.dynamic_slice_in_dim(query_column_scale, t * 512, 512, 0),
            lax.dynamic_slice_in_dim(key_value_column_scale, t * 128, 128, 0),
        ]
    )
    scale_out = lax.dynamic_slice_in_dim(output_column_scale, t * 512, 512, 0)

    received, ups, ups_out, scale_qkv, scale_out = lax.optimization_barrier(
        (received, ups, ups_out, scale_qkv, scale_out)
    )
    own_a, own_b, own_o, down_own, sums = unpack_columns(received, ups, ups_out)

    sums = sums.reshape(1152)
    sums = [sums] + [from_y(sums, step) for step in (1, 2, 3)]
    own_a, own_b, pair, sums = lax.optimization_barrier((own_a, own_b, pair, sums))

    next_a, last_a = from_y(own_a, 1), from_y(own_a, 3)
    tokens = [pair] + [from_x(pair, step) for step in (1, 2, 3)]
    next_a, last_a, tokens, late_b = lax.optimization_barrier((next_a, last_a, tokens, own_b))
    next_b, last_b = from_y(late_b, 1), from_y(late_b, 3)
    near = jnp.stack(tokens)
    far = swap_core(near)
    squares = token_sums(near).reshape(512)
    both = jnp.concatenate([sum(sums), squares + swap_core(squares)])
    both = both + swap_low(both)
    near, far, both, next_a, next_b, last_a, last_b = lax.optimization_barrier(
        (near, far, both, next_a, next_b, last_a, last_b)
    )
    far_a, far_b = from_y(next_a, 1), from_y(last_b, 3)
    factor_qkv = (scale_qkv / jnp.sqrt(both[:640])).reshape(1, 640)
    factor_out = (scale_out / jnp.sqrt(both[640:1152])).reshape(1, 512)
    inverse = lax.rsqrt(both[1152:] / 8192.0 + EPSILON).reshape(512, 1)
    weight_a, weight_b = scale_rows(own_o, down_own, ups_out, factor_out)

    gains = pick(input_norm_gain.reshape(4, 2, 2, 1, 512), zl, 1)

    def project(steps, blocks, total):
        place = [(y + step - x) % 4 for step in steps] + [(y + step) % 4 for step in steps]
        place = jnp.stack(place + [c, zh ^ zl]).astype(jnp.int32)
        return multiply_slabs(
            place, near, far, inverse, gains, blocks, ups, factor_qkv, total
        )

    total = project((0, 1, 3), (own_a, own_b, next_a, next_b, last_a, last_b), None)
    total, far_a, far_b, weight_a, weight_b = lax.optimization_barrier(
        (total, far_a, far_b, weight_a, weight_b)
    )
    other, mine = project((2,), (far_a, far_b), total)

    rows_o = [weight_a, weight_b, from_y(weight_a, 1), from_y(weight_b, 1)]
    rows_last = [from_y(weight_a, 3), from_y(weight_b, 3)]
    rows_o += [from_y(rows_o[2], 1), from_y(rows_last[1], 3)] + rows_last

    projected = (mine + swap_low(other)).astype(bf16).reshape(16, 16, 640)
    every = lax.all_to_all(projected, "tp", 0, 0, tiled=True)
    place = jnp.stack([y, zl]).astype(jnp.int32)
    attended = attend(place, lengths, every, cached_key_rows, cached_value_rows)

    attended, rows_o = lax.optimization_barrier((attended, rows_o))
    slabs = attended.reshape(2, 4, 16, 1024)

    def along_z(own, other):
        def flip(value, dl, dh):
            return permute(value, lambda y, zl, x, zh, c: (y, zl ^ dl, x, zh ^ dh, c))

        return jnp.stack([own, flip(own, 0, 1), flip(other, 1, 0), flip(other, 1, 1)])

    def along_x(value):
        return jnp.stack([value] + [from_x(value, step) for step in (1, 2, 3)])

    first = jnp.stack([slabs[0, :2], swap_low(slabs[1, :2])])
    flipped = permute(first, lambda y, zl, x, zh, c: (y, zl, x, 1 - zh, c))
    first = jnp.stack([first[0], flipped[0], first[1], flipped[1]])
    second = along_x(slabs[:, 2:])
    first = along_x(first)
    second = along_z(second[:, 0], second[:, 1])
    place = jnp.stack([x, zh, c]).astype(jnp.int32)
    mine, other = multiply_output(
        place, (first, second, swap_core(first), swap_core(second)), rows_o
    )
    result = (mine + swap_low(other).astype(f32)).astype(bf16)
    return result.reshape(16, 4, 4, 512).transpose(2, 0, 1, 3).reshape(4, 64, 512)


def solution(mesh):
    return jax.shard_map(
        per_device,
        mesh=mesh,
        in_specs=(
            P(None, "rep", "tp"),
            P(),
            P(("rep", "tp"), None),
            P(("rep", "tp"), None),
            P(("rep", "tp"), None),
            P(("rep", "tp"), None),
            P(),
            P(("rep", "tp"), None),
            P(),
            P(("rep", "tp"), None),
            P(),
            P(),
            P(),
            P(),
            P(("rep", "tp"), None, None, None),
            P(("rep", "tp"), None, None, None),
            P(("rep", "tp")),
        ),
        out_specs=P(None, "rep", "tp"),
        check_vma=False,
    )
```

```python
import math

import jax
import jax.numpy as jnp
from jax import lax
from jax.experimental import pallas as pl
from jax.experimental.pallas import tpu as pltpu
from jax.sharding import PartitionSpec as P

EPSILON = 1e-06
NEG_LARGE = -1e30
AXES = ("rep", "tp")


def device_index(y, zl, x, zh, c):
    return (y * 2 + zl) * 16 + x * 4 + zh * 2 + c


def permute(value, target):
    pairs = []
    for y in range(4):
        for zl in range(2):
            for x in range(4):
                for zh in range(2):
                    for c in range(2):
                        pairs.append(
                            (device_index(y, zl, x, zh, c), device_index(*target(y, zl, x, zh, c)))
                        )
    return lax.ppermute(value, AXES, pairs)


def swap_low(value):
    return permute(value, lambda y, zl, x, zh, c: (y, 1 - zl, x, zh, c))


def swap_core(value):
    return permute(value, lambda y, zl, x, zh, c: (y, zl, x, zh, 1 - c))


def from_y(value, step):
    return permute(value, lambda y, zl, x, zh, c: ((y - step) % 4, zl, x, zh, c))


def from_x(value, step):
    return permute(value, lambda y, zl, x, zh, c: (y, zl, (x - step) % 4, zh, c))


def after(value, earlier):
    return lax.optimization_barrier((value, earlier))[0]


def pick(value, index, axis=0):
    return lax.dynamic_index_in_dim(value, index, axis, keepdims=False)


def share_sums(sums):
    spread = jnp.broadcast_to(sums[None, :], (8, sums.shape[0]))
    return jnp.sum(lax.all_to_all(spread, "rep", 0, 0, tiled=True), axis=0)


def pack_columns_kernel(place, query, key_value, output, down_q, down_kv, down_o, out):
    f32 = jnp.float32
    down_q, down_kv, down_o = (d[...].astype(f32) for d in (down_q, down_kv, down_o))
    blank = jnp.zeros_like(down_o)
    down = jnp.where(
        place[0] < 8,
        jnp.concatenate([down_q, down_kv, down_o, blank], axis=0),
        jnp.concatenate([down_o, blank, down_q, down_kv], axis=0),
    )
    down = down.T.astype(jnp.bfloat16)
    for i in range(4):
        for k in range(4):
            columns = slice((i * 4 + k) * 128, (i * 4 + k + 1) * 128)
            out[i, k] = query[:, columns]
            out[i, 6 + k] = output[:, columns]
        out[i, 4] = key_value[:, i * 128 : (i + 1) * 128]
        out[i, 5] = down


def pack_columns(place, query, key_value, output, *downs):
    down = pl.BlockSpec((32, 64), lambda i, place: (0, 0))
    return pl.pallas_call(
        pack_columns_kernel,
        grid_spec=pltpu.PrefetchScalarGridSpec(
            num_scalar_prefetch=1,
            grid=(4,),
            in_specs=[
                pl.BlockSpec((64, 2048), lambda i, place: (0, i)),
                pl.BlockSpec((64, 512), lambda i, place: (0, i)),
                pl.BlockSpec((64, 2048), lambda i, place: (0, i)),
                down,
                down,
                down,
            ],
            out_specs=pl.BlockSpec((4, 10, 64, 128), lambda i, place: (i, 0, 0, 0)),
        ),
        out_shape=jax.ShapeDtypeStruct((16, 10, 64, 128), jnp.bfloat16),
        cost_estimate=pl.CostEstimate(flops=0, bytes_accessed=2**22, transcendentals=0),
    )(place, query, key_value, output, *downs)


def unpack_columns_kernel(received, ups, ups_out, block_a, block_b, rows_out, down, out):
    lanes = lax.broadcasted_iota(jnp.int32, (64, 128), 1)
    for i in range(8):
        rows = slice(i * 64, (i + 1) * 64)
        first, second = received[i, 5], received[8 + i, 5]
        down[0, rows] = first
        down[1, rows] = second
        block_a[0, rows] = jnp.where(
            lanes < 64, first.astype(jnp.float32), second.astype(jnp.float32)
        ).astype(jnp.bfloat16)
        for k in range(5):
            block_a[1 + k, rows] = received[i, k]
            block_b[k, rows] = received[8 + i, k]
        for k in range(4):
            for half in range(2):
                rows_out[half, rows, k * 128 : (k + 1) * 128] = received[half * 8 + i, 6 + k]
    total = None
    for half in range(2):
        merged = jnp.dot(block_a[0], ups[half], preferred_element_type=jnp.float32)
        sums = []
        for k in range(5):
            rows = block_a[1 + k] if half == 0 else block_b[k]
            tile = merged[:, k * 128 : (k + 1) * 128] + rows.astype(jnp.float32)
            sums.append(jnp.sum(tile * tile, axis=0, keepdims=True))
        merged = jnp.dot(down[half], ups_out[half], preferred_element_type=jnp.float32)
        merged = merged + rows_out[half].astype(jnp.float32)
        sums.append(jnp.sum(merged * merged, axis=0, keepdims=True))
        sums = jnp.concatenate(sums, axis=1)
        total = sums if total is None else total + sums
    out[...] = total


def unpack_columns(received, ups, ups_out):
    return pl.pallas_call(
        unpack_columns_kernel,
        out_shape=[
            jax.ShapeDtypeStruct((6, 512, 128), jnp.bfloat16),
            jax.ShapeDtypeStruct((5, 512, 128), jnp.bfloat16),
            jax.ShapeDtypeStruct((2, 512, 512), jnp.bfloat16),
            jax.ShapeDtypeStruct((2, 512, 128), jnp.bfloat16),
            jax.ShapeDtypeStruct((1, 1152), jnp.float32),
        ],
        compiler_params=pltpu.CompilerParams(vmem_limit_bytes=24 * 2**20),
        cost_estimate=pl.CostEstimate(flops=2**28, bytes_accessed=2**22, transcendentals=0),
    )(received, ups, ups_out)


def scale_rows_kernel(rows, down, ups, factor, out_a, out_b):
    for half, out in enumerate((out_a, out_b)):
        merged = jnp.dot(down[half], ups[half], preferred_element_type=jnp.float32)
        merged = rows[half].astype(jnp.float32) + merged
        out[...] = (merged * factor[...]).astype(jnp.bfloat16)


def scale_rows(rows, down, ups, factor):
    return pl.pallas_call(
        scale_rows_kernel,
        out_shape=[jax.ShapeDtypeStruct((512, 512), jnp.bfloat16)] * 2,
        compiler_params=pltpu.CompilerParams(vmem_limit_bytes=56 * 2**20),
        cost_estimate=pl.CostEstimate(flops=2**20, bytes_accessed=2**12, transcendentals=0),
    )(rows, down, ups, factor)


def token_sums_kernel(near, out):
    total = None
    for e in range(4):
        wide = near[e].astype(jnp.float32)
        part = jnp.sum(wide * wide, axis=1, keepdims=True)
        total = part if total is None else total + part
    out[...] = total


def token_sums(near):
    return pl.pallas_call(
        token_sums_kernel,
        out_shape=jax.ShapeDtypeStruct((512, 1), jnp.float32),
        compiler_params=pltpu.CompilerParams(vmem_limit_bytes=56 * 2**20),
        cost_estimate=pl.CostEstimate(flops=2**20, bytes_accessed=2**12, transcendentals=0),
    )(near)


def multiply_slabs_kernel(place, *refs):
    count = (place.shape[0] - 2) // 2
    slabs, refs = refs[: 3 * count], refs[3 * count :]
    inverse, ups, factor = refs[:3]
    blocks, rest = refs[3 : 3 + 2 * count], refs[3 + 2 * count :]
    value = None
    for i in range(count):
        near, far, gain = slabs[3 * i : 3 * i + 3]
        block_a, block_b = blocks[2 * i : 2 * i + 2]
        for half in range(2):
            tokens = jnp.where(place[2 * count] == half, near[0], far[0]).astype(jnp.float32)
            normed = (tokens * inverse[...] * gain[0, half]).astype(jnp.bfloat16)
            merged = jnp.dot(block_a[0], ups[half], preferred_element_type=jnp.float32)
            tiles = []
            for k in range(5):
                rows = block_a[1 + k] if half == 0 else block_b[k]
                tiles.append(merged[:, k * 128 : (k + 1) * 128] + rows.astype(jnp.float32))
            weight = (jnp.concatenate(tiles, axis=1) * factor[...]).astype(jnp.bfloat16)
            part = jnp.dot(normed, weight, preferred_element_type=jnp.float32)
            value = part if value is None else value + part
    if len(rest) == 1:
        rest[0][...] = value
    else:
        value = value + rest[0][...]
        swapped = place[2 * count + 1] == 1
        rest[1][:256] = jnp.where(swapped, value[256:], value[:256])
        rest[1][256:] = jnp.where(swapped, value[:256], value[256:])


def multiply_slabs(place, near, far, inverse, gains, blocks, ups, factor, total):
    count = len(blocks) // 2

    def whole(shape):
        return pl.BlockSpec(shape, lambda i, place: (0,) * len(shape))

    operands, specs = [], []
    for k in range(count):
        operands += [near, far, gains]
        specs += [pl.BlockSpec((1, 512, 512), lambda i, place, k=k: (place[k], 0, 0))] * 2
        specs.append(
            pl.BlockSpec((1, 2, 1, 512), lambda i, place, k=k: (place[count + k], 0, 0, 0))
        )
    rest = [inverse, ups, factor, *blocks] + ([] if total is None else [total])
    operands += rest
    specs += [whole(operand.shape) for operand in rest]
    return pl.pallas_call(
        multiply_slabs_kernel,
        grid_spec=pltpu.PrefetchScalarGridSpec(
            num_scalar_prefetch=1,
            grid=(1,),
            in_specs=specs,
            out_specs=whole((512, 640)),
        ),
        out_shape=jax.ShapeDtypeStruct((512, 640), jnp.float32),
        compiler_params=pltpu.CompilerParams(vmem_limit_bytes=56 * 2**20),
        cost_estimate=pl.CostEstimate(
            flops=2**20, bytes_accessed=2**12, transcendentals=0
        ),
    )(place, *operands)


def attend_kernel(place, lengths, every, keys, values, out):
    f32, bf16 = jnp.float32, jnp.bfloat16
    inv_root = 1.0 / math.sqrt(128)
    both = every[...].astype(f32)
    fresh_keys = every[0, :, 512:]
    fresh_values = every[1, :, 512:]
    contract_last = (((1,), (1,)), ((), ()))
    fresh_column = lax.broadcasted_iota(jnp.int32, (128, 16), 1)
    fresh_row = lax.broadcasted_iota(jnp.int32, (128, 16), 0)
    slots = lax.broadcasted_iota(jnp.int32, (32, 1024), 1)
    blank = jnp.zeros((32, 128), bf16)
    queries = [
        jnp.concatenate(
            [
                both[h // 4, b * 4 : b * 4 + 4, (h % 4) * 128 : (h % 4 + 1) * 128]
                for h in range(8)
            ],
            axis=0,
        ).astype(bf16)
        for b in range(4)
    ]
    fresh = lax.dot_general(
        jnp.concatenate(queries, axis=0), fresh_keys, contract_last, preferred_element_type=f32
    )
    own = (fresh_row // 32) * 4
    order = (fresh_column >= own) & (fresh_column - own <= fresh_row % 4)
    fresh = jnp.where(order, fresh * inv_root, NEG_LARGE)
    scores = []
    for b in (0, 2):
        query = jnp.concatenate(
            [
                jnp.concatenate([queries[b], blank], axis=1),
                jnp.concatenate([blank, queries[b + 1]], axis=1),
            ],
            axis=0,
        )
        key = jnp.concatenate([keys[b, 0], keys[b + 1, 0]], axis=1)
        scores.append(
            lax.dot_general(query, key, contract_last, preferred_element_type=f32)
        )
    live = jnp.concatenate([slots < lengths[b] for b in range(4)], axis=0)
    scores = jnp.where(live, jnp.concatenate(scores, axis=0) * inv_root, NEG_LARGE)
    peak = jnp.maximum(
        jnp.max(scores, axis=1, keepdims=True), jnp.max(fresh, axis=1, keepdims=True)
    )
    probs = jnp.where(live, jnp.exp(scores - peak), 0.0)
    fresh_probs = jnp.where(order, jnp.exp(fresh - peak), 0.0)
    total = jnp.sum(probs, axis=1, keepdims=True) + jnp.sum(fresh_probs, axis=1, keepdims=True)
    rounded = probs.astype(bf16)
    contexts = []
    for b in (0, 2):
        value = jnp.concatenate([values[b, 0], values[b + 1, 0]], axis=1)
        part = jnp.dot(rounded[b * 32 : b * 32 + 64], value, preferred_element_type=f32)
        contexts += [part[:32, :128], part[32:, 128:]]
    context = jnp.concatenate(contexts, axis=0)
    context += jnp.dot(fresh_probs.astype(bf16), fresh_values, preferred_element_type=f32)
    context = context / total
    pieces = [
        jnp.concatenate(
            [context[b * 32 + h * 4 : b * 32 + h * 4 + 4] for h in range(8)], axis=1
        )
        for b in range(4)
    ]
    out[0] = jnp.concatenate(pieces, axis=0).astype(bf16)


def attend(place, lengths, every, cached_key_rows, cached_value_rows):
    def slab(g, place, lengths):
        return (((g + place[1]) % 2) * 4 + (g // 2 + 4 - place[0]) % 4, 0, 0)

    cache = pl.BlockSpec((4, 1, 1024, 128), lambda g, place, lengths: (0, g, 0, 0))
    return pl.pallas_call(
        attend_kernel,
        grid_spec=pltpu.PrefetchScalarGridSpec(
            num_scalar_prefetch=2,
            grid=(8,),
            in_specs=[
                pl.BlockSpec((2, 16, 640), lambda g, place, lengths: (g, 0, 0)),
                cache,
                cache,
            ],
            out_specs=pl.BlockSpec((1, 16, 1024), slab),
        ),
        out_shape=jax.ShapeDtypeStruct((8, 16, 1024), jnp.bfloat16),
        compiler_params=pltpu.CompilerParams(vmem_limit_bytes=56 * 2**20),
        cost_estimate=pl.CostEstimate(flops=2**20, bytes_accessed=2**12, transcendentals=0),
    )(place, lengths, every, cached_key_rows, cached_value_rows)


def output_kernel(place, near_a, near_b, far_a, far_b, *refs):
    weights, (mine, other) = refs[:8], refs[8:]
    total = None
    for j in range(4):
        parts = []
        for first, second in ((near_a, near_b), (far_a, far_b)):
            if j < 2:
                parts.append(first[:, :, j].reshape(256, 1024))
            else:
                parts.extend(second[:, e, j - 2].reshape(64, 1024) for e in range(4))
        rows = jnp.concatenate(parts, axis=0)
        for half in range(2):
            part = jnp.dot(
                rows[:, half * 512 : (half + 1) * 512],
                weights[2 * j + half][...],
                preferred_element_type=jnp.float32,
            )
            total = part if total is None else total + part
    for cr in range(2):
        for e in range(4):
            for dl in range(2):
                for dh in range(2):
                    start = cr * 256 + e * 64 + dl * 32 + dh * 16
                    target = ((place[0] + e) % 4) * 4 + (place[1] ^ dh) * 2 + (place[2] ^ cr)
                    rows = total[start : start + 16]
                    if dl == 0:
                        mine[target] = rows
                    else:
                        other[target] = rows.astype(jnp.bfloat16)


def multiply_output(place, pieces, rows_o):
    def whole(shape):
        return pl.BlockSpec(shape, lambda i, place: (0,) * len(shape))

    operands = [*pieces, *rows_o]
    return pl.pallas_call(
        output_kernel,
        grid_spec=pltpu.PrefetchScalarGridSpec(
            num_scalar_prefetch=1,
            grid=(1,),
            in_specs=[whole(operand.shape) for operand in operands],
            out_specs=[whole((16, 16, 512)), whole((16, 16, 512))],
        ),
        out_shape=[
            jax.ShapeDtypeStruct((16, 16, 512), jnp.float32),
            jax.ShapeDtypeStruct((16, 16, 512), jnp.bfloat16),
        ],
        compiler_params=pltpu.CompilerParams(vmem_limit_bytes=40 * 2**20),
        cost_estimate=pl.CostEstimate(flops=2**31, bytes_accessed=2**23, transcendentals=0),
    )(place, *operands)


def per_device(
    token_hidden_rows,
    input_norm_gain,
    frozen_query,
    frozen_key_value,
    frozen_output,
    query_down_factor,
    query_up_factor,
    key_value_down_factor,
    key_value_up_factor,
    output_down_factor,
    output_up_factor,
    query_column_scale,
    key_value_column_scale,
    output_column_scale,
    cached_key_rows,
    cached_value_rows,
    lengths,
):
    f32, bf16 = jnp.float32, jnp.bfloat16
    r, t = lax.axis_index("rep"), lax.axis_index("tp")
    y, zl = r // 2, r % 2
    x, zh, c = t // 4, (t // 2) % 2, t % 2

    local = token_hidden_rows.transpose(1, 0, 2).reshape(256, 512)
    pair = jnp.concatenate(
        [
            permute(local, lambda y, zl, x, zh, c, s=s: (y, zh, x, zl ^ s, c))
            for s in range(2)
        ]
    )

    frozen = pack_columns(
        t.astype(jnp.int32).reshape(1),
        frozen_query,
        frozen_key_value,
        frozen_output,
        query_down_factor.T,
        key_value_down_factor.T,
        output_down_factor.T,
    )
    received = lax.all_to_all(frozen, "tp", 0, 0, tiled=True)

    up_q = lax.dynamic_slice_in_dim(query_up_factor, t * 512, 512, 1)
    up_kv = lax.dynamic_slice_in_dim(key_value_up_factor, t * 128, 128, 1)
    up_o = lax.dynamic_slice_in_dim(output_up_factor, t * 512, 512, 1)
    up_qkv = jnp.concatenate(
        [
            jnp.concatenate([up_q, jnp.zeros((32, 128), bf16)], axis=1),
            jnp.concatenate([jnp.zeros((32, 512), bf16), up_kv], axis=1),
        ],
        axis=0,
    )
    blank = jnp.zeros((64, 640), bf16)
    ups = jnp.stack(
        [jnp.concatenate([up_qkv, blank], axis=0), jnp.concatenate([blank, up_qkv], axis=0)]
    )
    blank = jnp.zeros((32, 512), bf16)
    ups_out = jnp.stack(
        [
            jnp.concatenate([blank, blank, up_o, blank]),
            jnp.concatenate([up_o, blank, blank, blank]),
        ]
    )
    scale_qkv = jnp.concatenate(
        [
            lax.dynamic_slice_in_dim(query_column_scale, t * 512, 512, 0),
            lax.dynamic_slice_in_dim(key_value_column_scale, t * 128, 128, 0),
        ]
    )
    scale_out = lax.dynamic_slice_in_dim(output_column_scale, t * 512, 512, 0)

    received, ups, ups_out, scale_qkv, scale_out = lax.optimization_barrier(
        (received, ups, ups_out, scale_qkv, scale_out)
    )
    own_a, own_b, own_o, down_own, sums = unpack_columns(received, ups, ups_out)

    sums = sums.reshape(1152)
    sums = [sums] + [from_y(sums, step) for step in (1, 2, 3)]
    own_a, own_b, pair, sums = lax.optimization_barrier((own_a, own_b, pair, sums))

    next_a, last_b = from_y(own_a, 1), from_y(own_b, 3)
    next_b, last_a = from_y(own_b, 1), from_y(own_a, 3)
    tokens = [pair] + [from_x(pair, step) for step in (1, 2, 3)]
    next_a, next_b, last_a, last_b, tokens = lax.optimization_barrier(
        (next_a, next_b, last_a, last_b, tokens)
    )
    far_a, far_b = from_y(next_a, 1), from_y(last_b, 3)
    near = jnp.stack(tokens)
    far = swap_core(near)
    squares = token_sums(near).reshape(512)
    both = jnp.concatenate([sum(sums), squares + swap_core(squares)])
    both = both + swap_low(both)
    factor_qkv = (scale_qkv / jnp.sqrt(both[:640])).reshape(1, 640)
    factor_out = (scale_out / jnp.sqrt(both[640:1152])).reshape(1, 512)
    inverse = lax.rsqrt(both[1152:] / 8192.0 + EPSILON).reshape(512, 1)
    weight_a, weight_b = scale_rows(own_o, down_own, ups_out, factor_out)

    gains = pick(input_norm_gain.reshape(4, 2, 2, 1, 512), zl, 1)

    def project(steps, blocks, total):
        place = [(y + step - x) % 4 for step in steps] + [(y + step) % 4 for step in steps]
        place = jnp.stack(place + [c, zh]).astype(jnp.int32)
        return multiply_slabs(
            place, near, far, inverse, gains, blocks, ups, factor_qkv, total
        )

    total = project((0, 1, 3), (own_a, own_b, next_a, next_b, last_a, last_b), None)
    total, far_a, far_b, weight_a, weight_b = lax.optimization_barrier(
        (total, far_a, far_b, weight_a, weight_b)
    )
    total = project((2,), (far_a, far_b), total)

    rows_o = [weight_a, weight_b, from_y(weight_a, 1), from_y(weight_b, 1)]
    rows_last = [from_y(weight_a, 3), from_y(weight_b, 3)]

    groups = [[32 * k + i for i in range(32)] for k in range(4)]
    halves = lax.all_to_all(
        total.reshape(32, 16, 640), AXES, 0, 0, axis_index_groups=groups, tiled=True
    )
    every = jnp.sum(halves.reshape(2, 16, 16, 640), axis=0).astype(bf16)
    rows_next, rows_before, every = lax.optimization_barrier((rows_o[2], rows_last[1], every))
    rows_o += [from_y(rows_next, 1), from_y(rows_before, 3)] + rows_last

    place = jnp.stack([y, zl]).astype(jnp.int32)
    attended = attend(place, lengths, every, cached_key_rows, cached_value_rows)

    attended, rows_o = lax.optimization_barrier((attended, rows_o))
    slabs = attended.reshape(2, 4, 16, 1024)

    def along_z(own, other):
        def flip(value, dl, dh):
            return permute(value, lambda y, zl, x, zh, c: (y, zl ^ dl, x, zh ^ dh, c))

        return jnp.stack([own, flip(own, 0, 1), flip(other, 1, 0), flip(other, 1, 1)])

    def along_x(value):
        return jnp.stack([value] + [from_x(value, step) for step in (1, 2, 3)])

    first = jnp.stack([slabs[0, :2], swap_low(slabs[1, :2])])
    flipped = permute(first, lambda y, zl, x, zh, c: (y, zl, x, 1 - zh, c))
    first = jnp.stack([first[0], flipped[0], first[1], flipped[1]])
    second = along_x(slabs[:, 2:])
    first = along_x(first)
    second = along_z(second[:, 0], second[:, 1])
    place = jnp.stack([x, zh, c]).astype(jnp.int32)
    mine, other = multiply_output(
        place, (first, second, swap_core(first), swap_core(second)), rows_o
    )
    result = (mine + swap_low(other).astype(f32)).astype(bf16)
    return result.reshape(16, 4, 4, 512).transpose(2, 0, 1, 3).reshape(4, 64, 512)


def solution(mesh):
    return jax.shard_map(
        per_device,
        mesh=mesh,
        in_specs=(
            P(None, "rep", "tp"),
            P(),
            P(("rep", "tp"), None),
            P(("rep", "tp"), None),
            P(("rep", "tp"), None),
            P(("rep", "tp"), None),
            P(),
            P(("rep", "tp"), None),
            P(),
            P(("rep", "tp"), None),
            P(),
            P(),
            P(),
            P(),
            P(("rep", "tp"), None, None, None),
            P(("rep", "tp"), None, None, None),
            P(("rep", "tp")),
        ),
        out_specs=P(None, "rep", "tp"),
        check_vma=False,
    )
```

```python
import math

import jax
import jax.numpy as jnp
from jax import lax
from jax.experimental import pallas as pl
from jax.experimental.pallas import tpu as pltpu
from jax.sharding import PartitionSpec as P

EPSILON = 1e-06
NEG_LARGE = -1e30
AXES = ("rep", "tp")


def device_index(y, zl, x, zh, c):
    return (y * 2 + zl) * 16 + x * 4 + zh * 2 + c


def permute(value, target):
    pairs = []
    for y in range(4):
        for zl in range(2):
            for x in range(4):
                for zh in range(2):
                    for c in range(2):
                        pairs.append(
                            (device_index(y, zl, x, zh, c), device_index(*target(y, zl, x, zh, c)))
                        )
    return lax.ppermute(value, AXES, pairs)


def swap_low(value):
    return permute(value, lambda y, zl, x, zh, c: (y, 1 - zl, x, zh, c))


def swap_core(value):
    return permute(value, lambda y, zl, x, zh, c: (y, zl, x, zh, 1 - c))


def from_y(value, step):
    return permute(value, lambda y, zl, x, zh, c: ((y - step) % 4, zl, x, zh, c))


def from_x(value, step):
    return permute(value, lambda y, zl, x, zh, c: (y, zl, (x - step) % 4, zh, c))


def after(value, earlier):
    return lax.optimization_barrier((value, earlier))[0]


def pick(value, index, axis=0):
    return lax.dynamic_index_in_dim(value, index, axis, keepdims=False)


def share_sums(sums):
    spread = jnp.broadcast_to(sums[None, :], (8, sums.shape[0]))
    return jnp.sum(lax.all_to_all(spread, "rep", 0, 0, tiled=True), axis=0)


def pack_columns_kernel(place, query, key_value, output, down_q, down_kv, down_o, out):
    f32 = jnp.float32
    down_q, down_kv, down_o = (d[...].astype(f32) for d in (down_q, down_kv, down_o))
    blank = jnp.zeros_like(down_o)
    down = jnp.where(
        place[0] < 8,
        jnp.concatenate([down_q, down_kv, down_o, blank], axis=0),
        jnp.concatenate([down_o, blank, down_q, down_kv], axis=0),
    )
    down = down.T.astype(jnp.bfloat16)
    for i in range(4):
        for k in range(4):
            columns = slice((i * 4 + k) * 128, (i * 4 + k + 1) * 128)
            out[i, k] = query[:, columns]
            out[i, 6 + k] = output[:, columns]
        out[i, 4] = key_value[:, i * 128 : (i + 1) * 128]
        out[i, 5] = down


def pack_columns(place, query, key_value, output, *downs):
    down = pl.BlockSpec((32, 64), lambda i, place: (0, 0))
    return pl.pallas_call(
        pack_columns_kernel,
        grid_spec=pltpu.PrefetchScalarGridSpec(
            num_scalar_prefetch=1,
            grid=(4,),
            in_specs=[
                pl.BlockSpec((64, 2048), lambda i, place: (0, i)),
                pl.BlockSpec((64, 512), lambda i, place: (0, i)),
                pl.BlockSpec((64, 2048), lambda i, place: (0, i)),
                down,
                down,
                down,
            ],
            out_specs=pl.BlockSpec((4, 10, 64, 128), lambda i, place: (i, 0, 0, 0)),
        ),
        out_shape=jax.ShapeDtypeStruct((16, 10, 64, 128), jnp.bfloat16),
        cost_estimate=pl.CostEstimate(flops=0, bytes_accessed=2**22, transcendentals=0),
    )(place, query, key_value, output, *downs)


def unpack_columns_kernel(received, ups, ups_out, block_a, block_b, rows_out, down, out):
    lanes = lax.broadcasted_iota(jnp.int32, (64, 128), 1)
    for i in range(8):
        rows = slice(i * 64, (i + 1) * 64)
        first, second = received[i, 5], received[8 + i, 5]
        down[0, rows] = first
        down[1, rows] = second
        block_a[0, rows] = jnp.where(
            lanes < 64, first.astype(jnp.float32), second.astype(jnp.float32)
        ).astype(jnp.bfloat16)
        for k in range(5):
            block_a[1 + k, rows] = received[i, k]
            block_b[k, rows] = received[8 + i, k]
        for k in range(4):
            for half in range(2):
                rows_out[half, rows, k * 128 : (k + 1) * 128] = received[half * 8 + i, 6 + k]
    total = None
    for half in range(2):
        merged = jnp.dot(block_a[0], ups[half], preferred_element_type=jnp.float32)
        sums = []
        for k in range(5):
            rows = block_a[1 + k] if half == 0 else block_b[k]
            tile = merged[:, k * 128 : (k + 1) * 128] + rows.astype(jnp.float32)
            sums.append(jnp.sum(tile * tile, axis=0, keepdims=True))
        merged = jnp.dot(down[half], ups_out[half], preferred_element_type=jnp.float32)
        merged = merged + rows_out[half].astype(jnp.float32)
        sums.append(jnp.sum(merged * merged, axis=0, keepdims=True))
        sums = jnp.concatenate(sums, axis=1)
        total = sums if total is None else total + sums
    out[...] = total


def unpack_columns(received, ups, ups_out):
    return pl.pallas_call(
        unpack_columns_kernel,
        out_shape=[
            jax.ShapeDtypeStruct((6, 512, 128), jnp.bfloat16),
            jax.ShapeDtypeStruct((5, 512, 128), jnp.bfloat16),
            jax.ShapeDtypeStruct((2, 512, 512), jnp.bfloat16),
            jax.ShapeDtypeStruct((2, 512, 128), jnp.bfloat16),
            jax.ShapeDtypeStruct((1, 1152), jnp.float32),
        ],
        compiler_params=pltpu.CompilerParams(vmem_limit_bytes=24 * 2**20),
        cost_estimate=pl.CostEstimate(flops=2**28, bytes_accessed=2**22, transcendentals=0),
    )(received, ups, ups_out)


def scale_rows_kernel(rows, down, ups, factor, out_a, out_b):
    for half, out in enumerate((out_a, out_b)):
        merged = jnp.dot(down[half], ups[half], preferred_element_type=jnp.float32)
        merged = rows[half].astype(jnp.float32) + merged
        out[...] = (merged * factor[...]).astype(jnp.bfloat16)


def scale_rows(rows, down, ups, factor):
    return pl.pallas_call(
        scale_rows_kernel,
        out_shape=[jax.ShapeDtypeStruct((512, 512), jnp.bfloat16)] * 2,
        compiler_params=pltpu.CompilerParams(vmem_limit_bytes=56 * 2**20),
        cost_estimate=pl.CostEstimate(flops=2**20, bytes_accessed=2**12, transcendentals=0),
    )(rows, down, ups, factor)


def token_sums_kernel(near, out):
    total = None
    for e in range(4):
        wide = near[e].astype(jnp.float32)
        part = jnp.sum(wide * wide, axis=1, keepdims=True)
        total = part if total is None else total + part
    out[...] = total


def token_sums(near):
    return pl.pallas_call(
        token_sums_kernel,
        out_shape=jax.ShapeDtypeStruct((512, 1), jnp.float32),
        compiler_params=pltpu.CompilerParams(vmem_limit_bytes=56 * 2**20),
        cost_estimate=pl.CostEstimate(flops=2**20, bytes_accessed=2**12, transcendentals=0),
    )(near)


def multiply_slabs_kernel(place, *refs):
    count = (place.shape[0] - 2) // 2
    slabs, refs = refs[: 3 * count], refs[3 * count :]
    inverse, ups, factor = refs[:3]
    blocks, rest = refs[3 : 3 + 2 * count], refs[3 + 2 * count :]
    value = None
    for i in range(count):
        near, far, gain = slabs[3 * i : 3 * i + 3]
        block_a, block_b = blocks[2 * i : 2 * i + 2]
        for half in range(2):
            tokens = jnp.where(place[2 * count] == half, near[0], far[0]).astype(jnp.float32)
            normed = (tokens * inverse[...] * gain[0, half]).astype(jnp.bfloat16)
            merged = jnp.dot(block_a[0], ups[half], preferred_element_type=jnp.float32)
            tiles = []
            for k in range(5):
                rows = block_a[1 + k] if half == 0 else block_b[k]
                tiles.append(merged[:, k * 128 : (k + 1) * 128] + rows.astype(jnp.float32))
            weight = (jnp.concatenate(tiles, axis=1) * factor[...]).astype(jnp.bfloat16)
            part = jnp.dot(normed, weight, preferred_element_type=jnp.float32)
            value = part if value is None else value + part
    if len(rest) == 1:
        rest[0][...] = value
    else:
        value = value + rest[0][...]
        swapped = place[2 * count + 1] == 1
        rest[1][:256] = jnp.where(swapped, value[256:], value[:256])
        rest[1][256:] = jnp.where(swapped, value[:256], value[256:])


def multiply_slabs(place, near, far, inverse, gains, blocks, ups, factor, total):
    count = len(blocks) // 2

    def whole(shape):
        return pl.BlockSpec(shape, lambda i, place: (0,) * len(shape))

    operands, specs = [], []
    for k in range(count):
        operands += [near, far, gains]
        specs += [pl.BlockSpec((1, 512, 512), lambda i, place, k=k: (place[k], 0, 0))] * 2
        specs.append(
            pl.BlockSpec((1, 2, 1, 512), lambda i, place, k=k: (place[count + k], 0, 0, 0))
        )
    rest = [inverse, ups, factor, *blocks] + ([] if total is None else [total])
    operands += rest
    specs += [whole(operand.shape) for operand in rest]
    return pl.pallas_call(
        multiply_slabs_kernel,
        grid_spec=pltpu.PrefetchScalarGridSpec(
            num_scalar_prefetch=1,
            grid=(1,),
            in_specs=specs,
            out_specs=whole((512, 640)),
        ),
        out_shape=jax.ShapeDtypeStruct((512, 640), jnp.float32),
        compiler_params=pltpu.CompilerParams(vmem_limit_bytes=56 * 2**20),
        cost_estimate=pl.CostEstimate(
            flops=2**20, bytes_accessed=2**12, transcendentals=0
        ),
    )(place, *operands)


def attend_kernel(place, lengths, every, keys, values, out):
    f32, bf16 = jnp.float32, jnp.bfloat16
    inv_root = 1.0 / math.sqrt(128)
    both = every[...].astype(f32)
    fresh_keys = every[0, :, 512:]
    fresh_values = every[1, :, 512:]
    contract_last = (((1,), (1,)), ((), ()))
    fresh_column = lax.broadcasted_iota(jnp.int32, (128, 16), 1)
    fresh_row = lax.broadcasted_iota(jnp.int32, (128, 16), 0)
    slots = lax.broadcasted_iota(jnp.int32, (32, 1024), 1)
    blank = jnp.zeros((32, 128), bf16)
    queries = [
        jnp.concatenate(
            [
                both[h // 4, b * 4 : b * 4 + 4, (h % 4) * 128 : (h % 4 + 1) * 128]
                for h in range(8)
            ],
            axis=0,
        ).astype(bf16)
        for b in range(4)
    ]
    fresh = lax.dot_general(
        jnp.concatenate(queries, axis=0), fresh_keys, contract_last, preferred_element_type=f32
    )
    own = (fresh_row // 32) * 4
    order = (fresh_column >= own) & (fresh_column - own <= fresh_row % 4)
    fresh = jnp.where(order, fresh * inv_root, NEG_LARGE)
    scores = []
    for b in (0, 2):
        query = jnp.concatenate(
            [
                jnp.concatenate([queries[b], blank], axis=1),
                jnp.concatenate([blank, queries[b + 1]], axis=1),
            ],
            axis=0,
        )
        key = jnp.concatenate([keys[b, 0], keys[b + 1, 0]], axis=1)
        scores.append(
            lax.dot_general(query, key, contract_last, preferred_element_type=f32)
        )
    live = jnp.concatenate([slots < lengths[b] for b in range(4)], axis=0)
    scores = jnp.where(live, jnp.concatenate(scores, axis=0) * inv_root, NEG_LARGE)
    peak = jnp.maximum(
        jnp.max(scores, axis=1, keepdims=True), jnp.max(fresh, axis=1, keepdims=True)
    )
    probs = jnp.where(live, jnp.exp(scores - peak), 0.0)
    fresh_probs = jnp.where(order, jnp.exp(fresh - peak), 0.0)
    total = jnp.sum(probs, axis=1, keepdims=True) + jnp.sum(fresh_probs, axis=1, keepdims=True)
    rounded = probs.astype(bf16)
    contexts = []
    for b in (0, 2):
        value = jnp.concatenate([values[b, 0], values[b + 1, 0]], axis=1)
        part = jnp.dot(rounded[b * 32 : b * 32 + 64], value, preferred_element_type=f32)
        contexts += [part[:32, :128], part[32:, 128:]]
    context = jnp.concatenate(contexts, axis=0)
    context += jnp.dot(fresh_probs.astype(bf16), fresh_values, preferred_element_type=f32)
    context = context / total
    pieces = [
        jnp.concatenate(
            [context[b * 32 + h * 4 : b * 32 + h * 4 + 4] for h in range(8)], axis=1
        )
        for b in range(4)
    ]
    out[0] = jnp.concatenate(pieces, axis=0).astype(bf16)


def attend(place, lengths, every, cached_key_rows, cached_value_rows):
    def slab(g, place, lengths):
        return (((g + place[1]) % 2) * 4 + (g // 2 + 4 - place[0]) % 4, 0, 0)

    cache = pl.BlockSpec((4, 1, 1024, 128), lambda g, place, lengths: (0, g, 0, 0))
    return pl.pallas_call(
        attend_kernel,
        grid_spec=pltpu.PrefetchScalarGridSpec(
            num_scalar_prefetch=2,
            grid=(8,),
            in_specs=[
                pl.BlockSpec((2, 16, 640), lambda g, place, lengths: (g, 0, 0)),
                cache,
                cache,
            ],
            out_specs=pl.BlockSpec((1, 16, 1024), slab),
        ),
        out_shape=jax.ShapeDtypeStruct((8, 16, 1024), jnp.bfloat16),
        compiler_params=pltpu.CompilerParams(vmem_limit_bytes=56 * 2**20),
        cost_estimate=pl.CostEstimate(flops=2**20, bytes_accessed=2**12, transcendentals=0),
    )(place, lengths, every, cached_key_rows, cached_value_rows)


def output_kernel(place, near_a, near_b, far_a, far_b, *refs):
    weights, (mine, other) = refs[:8], refs[8:]
    total = None
    for j in range(4):
        parts = []
        for first, second in ((near_a, near_b), (far_a, far_b)):
            if j < 2:
                parts.append(first[:, :, j].reshape(256, 1024))
            else:
                parts.extend(second[:, e, j - 2].reshape(64, 1024) for e in range(4))
        rows = jnp.concatenate(parts, axis=0)
        for half in range(2):
            part = jnp.dot(
                rows[:, half * 512 : (half + 1) * 512],
                weights[2 * j + half][...],
                preferred_element_type=jnp.float32,
            )
            total = part if total is None else total + part
    for cr in range(2):
        for e in range(4):
            for dl in range(2):
                for dh in range(2):
                    start = cr * 256 + e * 64 + dl * 32 + dh * 16
                    target = ((place[0] + e) % 4) * 4 + (place[1] ^ dh) * 2 + (place[2] ^ cr)
                    rows = total[start : start + 16]
                    if dl == 0:
                        mine[target] = rows
                    else:
                        other[target] = rows.astype(jnp.bfloat16)


def multiply_output(place, pieces, rows_o):
    def whole(shape):
        return pl.BlockSpec(shape, lambda i, place: (0,) * len(shape))

    operands = [*pieces, *rows_o]
    return pl.pallas_call(
        output_kernel,
        grid_spec=pltpu.PrefetchScalarGridSpec(
            num_scalar_prefetch=1,
            grid=(1,),
            in_specs=[whole(operand.shape) for operand in operands],
            out_specs=[whole((16, 16, 512)), whole((16, 16, 512))],
        ),
        out_shape=[
            jax.ShapeDtypeStruct((16, 16, 512), jnp.float32),
            jax.ShapeDtypeStruct((16, 16, 512), jnp.bfloat16),
        ],
        compiler_params=pltpu.CompilerParams(vmem_limit_bytes=40 * 2**20),
        cost_estimate=pl.CostEstimate(flops=2**31, bytes_accessed=2**23, transcendentals=0),
    )(place, *operands)


def per_device(
    token_hidden_rows,
    input_norm_gain,
    frozen_query,
    frozen_key_value,
    frozen_output,
    query_down_factor,
    query_up_factor,
    key_value_down_factor,
    key_value_up_factor,
    output_down_factor,
    output_up_factor,
    query_column_scale,
    key_value_column_scale,
    output_column_scale,
    cached_key_rows,
    cached_value_rows,
    lengths,
):
    f32, bf16 = jnp.float32, jnp.bfloat16
    r, t = lax.axis_index("rep"), lax.axis_index("tp")
    y, zl = r // 2, r % 2
    x, zh, c = t // 4, (t // 2) % 2, t % 2

    local = token_hidden_rows.transpose(1, 0, 2).reshape(256, 512)
    pair = jnp.concatenate(
        [
            permute(local, lambda y, zl, x, zh, c, s=s: (y, zh, x, zl ^ s, c))
            for s in range(2)
        ]
    )

    frozen = pack_columns(
        t.astype(jnp.int32).reshape(1),
        frozen_query,
        frozen_key_value,
        frozen_output,
        query_down_factor.T,
        key_value_down_factor.T,
        output_down_factor.T,
    )
    received = lax.all_to_all(frozen, "tp", 0, 0, tiled=True)

    up_q = lax.dynamic_slice_in_dim(query_up_factor, t * 512, 512, 1)
    up_kv = lax.dynamic_slice_in_dim(key_value_up_factor, t * 128, 128, 1)
    up_o = lax.dynamic_slice_in_dim(output_up_factor, t * 512, 512, 1)
    up_qkv = jnp.concatenate(
        [
            jnp.concatenate([up_q, jnp.zeros((32, 128), bf16)], axis=1),
            jnp.concatenate([jnp.zeros((32, 512), bf16), up_kv], axis=1),
        ],
        axis=0,
    )
    blank = jnp.zeros((64, 640), bf16)
    ups = jnp.stack(
        [jnp.concatenate([up_qkv, blank], axis=0), jnp.concatenate([blank, up_qkv], axis=0)]
    )
    blank = jnp.zeros((32, 512), bf16)
    ups_out = jnp.stack(
        [
            jnp.concatenate([blank, blank, up_o, blank]),
            jnp.concatenate([up_o, blank, blank, blank]),
        ]
    )
    scale_qkv = jnp.concatenate(
        [
            lax.dynamic_slice_in_dim(query_column_scale, t * 512, 512, 0),
            lax.dynamic_slice_in_dim(key_value_column_scale, t * 128, 128, 0),
        ]
    )
    scale_out = lax.dynamic_slice_in_dim(output_column_scale, t * 512, 512, 0)

    received, ups, ups_out, scale_qkv, scale_out = lax.optimization_barrier(
        (received, ups, ups_out, scale_qkv, scale_out)
    )
    own_a, own_b, own_o, down_own, sums = unpack_columns(received, ups, ups_out)

    sums = sums.reshape(1152)
    sums = [sums] + [from_y(sums, step) for step in (1, 2, 3)]
    own_a, own_b, pair, sums = lax.optimization_barrier((own_a, own_b, pair, sums))

    next_a, last_b = from_y(own_a, 1), from_y(own_b, 3)
    next_b, last_a = from_y(own_b, 1), from_y(own_a, 3)
    tokens = [pair] + [from_x(pair, step) for step in (1, 2, 3)]
    near = jnp.stack(tokens)
    next_a, next_b, last_a, last_b, near = lax.optimization_barrier(
        (next_a, next_b, last_a, last_b, near)
    )
    far_a, far_b = from_y(next_a, 1), from_y(last_b, 3)
    far = swap_core(near)
    squares = token_sums(near).reshape(512)
    both = jnp.concatenate([sum(sums), squares + swap_core(squares)])
    both = both + swap_low(both)
    factor_qkv = (scale_qkv / jnp.sqrt(both[:640])).reshape(1, 640)
    factor_out = (scale_out / jnp.sqrt(both[640:1152])).reshape(1, 512)
    inverse = lax.rsqrt(both[1152:] / 8192.0 + EPSILON).reshape(512, 1)
    weight_a, weight_b = scale_rows(own_o, down_own, ups_out, factor_out)

    gains = pick(input_norm_gain.reshape(4, 2, 2, 1, 512), zl, 1)

    def project(steps, blocks, total):
        place = [(y + step - x) % 4 for step in steps] + [(y + step) % 4 for step in steps]
        place = jnp.stack(place + [c, zh]).astype(jnp.int32)
        return multiply_slabs(
            place, near, far, inverse, gains, blocks, ups, factor_qkv, total
        )

    total = project((0, 1, 3), (own_a, own_b, next_a, next_b, last_a, last_b), None)
    total, far_a, far_b = lax.optimization_barrier((total, far_a, far_b))
    weight_a, weight_b = lax.optimization_barrier((weight_a, weight_b, far_a))[:2]
    total = project((2,), (far_a, far_b), total)

    rows_o = [weight_a, weight_b, from_y(weight_a, 1), from_y(weight_b, 1)]
    rows_last = [from_y(weight_a, 3), from_y(weight_b, 3)]

    groups = [[32 * k + i for i in range(32)] for k in range(4)]
    halves = lax.all_to_all(
        total.reshape(32, 16, 640), AXES, 0, 0, axis_index_groups=groups, tiled=True
    )
    every = jnp.sum(halves.reshape(2, 16, 16, 640), axis=0).astype(bf16)
    rows_next, rows_before, every = lax.optimization_barrier((rows_o[2], rows_last[1], every))
    rows_o += [from_y(rows_next, 1), from_y(rows_before, 3)] + rows_last

    place = jnp.stack([y, zl]).astype(jnp.int32)
    attended = attend(place, lengths, every, cached_key_rows, cached_value_rows)

    attended, rows_o = lax.optimization_barrier((attended, rows_o))
    slabs = attended.reshape(2, 4, 16, 1024)

    def along_z(own, other):
        def flip(value, dl, dh):
            return permute(value, lambda y, zl, x, zh, c: (y, zl ^ dl, x, zh ^ dh, c))

        return jnp.stack([own, flip(own, 0, 1), flip(other, 1, 0), flip(other, 1, 1)])

    def along_x(value):
        return jnp.stack([value] + [from_x(value, step) for step in (1, 2, 3)])

    first = jnp.stack([slabs[0, :2], swap_low(slabs[1, :2])])
    flipped = permute(first, lambda y, zl, x, zh, c: (y, zl, x, 1 - zh, c))
    first = jnp.stack([first[0], flipped[0], first[1], flipped[1]])
    second = along_x(slabs[:, 2:])
    first = along_x(first)
    second = along_z(second[:, 0], second[:, 1])
    place = jnp.stack([x, zh, c]).astype(jnp.int32)
    mine, other = multiply_output(
        place, (first, second, swap_core(first), swap_core(second)), rows_o
    )
    result = (mine + swap_low(other).astype(f32)).astype(bf16)
    return result.reshape(16, 4, 4, 512).transpose(2, 0, 1, 3).reshape(4, 64, 512)


def solution(mesh):
    return jax.shard_map(
        per_device,
        mesh=mesh,
        in_specs=(
            P(None, "rep", "tp"),
            P(),
            P(("rep", "tp"), None),
            P(("rep", "tp"), None),
            P(("rep", "tp"), None),
            P(("rep", "tp"), None),
            P(),
            P(("rep", "tp"), None),
            P(),
            P(("rep", "tp"), None),
            P(),
            P(),
            P(),
            P(),
            P(("rep", "tp"), None, None, None),
            P(("rep", "tp"), None, None, None),
            P(("rep", "tp")),
        ),
        out_specs=P(None, "rep", "tp"),
        check_vma=False,
    )
```

```python
import math

import jax
import jax.numpy as jnp
from jax import lax
from jax.experimental import pallas as pl
from jax.experimental.pallas import tpu as pltpu
from jax.sharding import PartitionSpec as P

EPSILON = 1e-06
NEG_LARGE = -1e30
AXES = ("rep", "tp")


def device_index(y, zl, x, zh, c):
    return (y * 2 + zl) * 16 + x * 4 + zh * 2 + c


def permute(value, target):
    pairs = []
    for y in range(4):
        for zl in range(2):
            for x in range(4):
                for zh in range(2):
                    for c in range(2):
                        pairs.append(
                            (device_index(y, zl, x, zh, c), device_index(*target(y, zl, x, zh, c)))
                        )
    return lax.ppermute(value, AXES, pairs)


def swap_low(value):
    return permute(value, lambda y, zl, x, zh, c: (y, 1 - zl, x, zh, c))


def swap_core(value):
    return permute(value, lambda y, zl, x, zh, c: (y, zl, x, zh, 1 - c))


def from_y(value, step):
    return permute(value, lambda y, zl, x, zh, c: ((y - step) % 4, zl, x, zh, c))


def from_x(value, step):
    return permute(value, lambda y, zl, x, zh, c: (y, zl, (x - step) % 4, zh, c))


def after(value, earlier):
    return lax.optimization_barrier((value, earlier))[0]


def pick(value, index, axis=0):
    return lax.dynamic_index_in_dim(value, index, axis, keepdims=False)


def share_sums(sums):
    spread = jnp.broadcast_to(sums[None, :], (8, sums.shape[0]))
    return jnp.sum(lax.all_to_all(spread, "rep", 0, 0, tiled=True), axis=0)


def pack_columns_kernel(place, query, key_value, output, down_q, down_kv, down_o, out):
    f32 = jnp.float32
    down_q, down_kv, down_o = (d[...].astype(f32) for d in (down_q, down_kv, down_o))
    blank = jnp.zeros_like(down_o)
    down = jnp.where(
        place[0] < 8,
        jnp.concatenate([down_q, down_kv, down_o, blank], axis=0),
        jnp.concatenate([down_o, blank, down_q, down_kv], axis=0),
    )
    down = down.T.astype(jnp.bfloat16)
    for i in range(4):
        for k in range(4):
            columns = slice((i * 4 + k) * 128, (i * 4 + k + 1) * 128)
            out[i, k] = query[:, columns]
            out[i, 6 + k] = output[:, columns]
        out[i, 4] = key_value[:, i * 128 : (i + 1) * 128]
        out[i, 5] = down


def pack_columns(place, query, key_value, output, *downs):
    down = pl.BlockSpec((32, 64), lambda i, place: (0, 0))
    return pl.pallas_call(
        pack_columns_kernel,
        grid_spec=pltpu.PrefetchScalarGridSpec(
            num_scalar_prefetch=1,
            grid=(4,),
            in_specs=[
                pl.BlockSpec((64, 2048), lambda i, place: (0, i)),
                pl.BlockSpec((64, 512), lambda i, place: (0, i)),
                pl.BlockSpec((64, 2048), lambda i, place: (0, i)),
                down,
                down,
                down,
            ],
            out_specs=pl.BlockSpec((4, 10, 64, 128), lambda i, place: (i, 0, 0, 0)),
        ),
        out_shape=jax.ShapeDtypeStruct((16, 10, 64, 128), jnp.bfloat16),
        cost_estimate=pl.CostEstimate(flops=0, bytes_accessed=2**22, transcendentals=0),
    )(place, query, key_value, output, *downs)


def unpack_columns_kernel(received, ups, ups_out, block_a, block_b, rows_out, down, out):
    lanes = lax.broadcasted_iota(jnp.int32, (64, 128), 1)
    for i in range(8):
        rows = slice(i * 64, (i + 1) * 64)
        first, second = received[i, 5], received[8 + i, 5]
        down[0, rows] = first
        down[1, rows] = second
        block_a[0, rows] = jnp.where(
            lanes < 64, first.astype(jnp.float32), second.astype(jnp.float32)
        ).astype(jnp.bfloat16)
        for k in range(5):
            block_a[1 + k, rows] = received[i, k]
            block_b[k, rows] = received[8 + i, k]
        for k in range(4):
            for half in range(2):
                rows_out[half, rows, k * 128 : (k + 1) * 128] = received[half * 8 + i, 6 + k]
    total = None
    for half in range(2):
        merged = jnp.dot(block_a[0], ups[half], preferred_element_type=jnp.float32)
        sums = []
        for k in range(5):
            rows = block_a[1 + k] if half == 0 else block_b[k]
            tile = merged[:, k * 128 : (k + 1) * 128] + rows.astype(jnp.float32)
            sums.append(jnp.sum(tile * tile, axis=0, keepdims=True))
        merged = jnp.dot(down[half], ups_out[half], preferred_element_type=jnp.float32)
        merged = merged + rows_out[half].astype(jnp.float32)
        sums.append(jnp.sum(merged * merged, axis=0, keepdims=True))
        sums = jnp.concatenate(sums, axis=1)
        total = sums if total is None else total + sums
    out[...] = total


def unpack_columns(received, ups, ups_out):
    return pl.pallas_call(
        unpack_columns_kernel,
        out_shape=[
            jax.ShapeDtypeStruct((6, 512, 128), jnp.bfloat16),
            jax.ShapeDtypeStruct((5, 512, 128), jnp.bfloat16),
            jax.ShapeDtypeStruct((2, 512, 512), jnp.bfloat16),
            jax.ShapeDtypeStruct((2, 512, 128), jnp.bfloat16),
            jax.ShapeDtypeStruct((1, 1152), jnp.float32),
        ],
        compiler_params=pltpu.CompilerParams(vmem_limit_bytes=24 * 2**20),
        cost_estimate=pl.CostEstimate(flops=2**28, bytes_accessed=2**22, transcendentals=0),
    )(received, ups, ups_out)


def scale_rows_kernel(rows, down, ups, factor, out_a, out_b):
    for half, out in enumerate((out_a, out_b)):
        merged = jnp.dot(down[half], ups[half], preferred_element_type=jnp.float32)
        merged = rows[half].astype(jnp.float32) + merged
        out[...] = (merged * factor[...]).astype(jnp.bfloat16)


def scale_rows(rows, down, ups, factor):
    return pl.pallas_call(
        scale_rows_kernel,
        out_shape=[jax.ShapeDtypeStruct((512, 512), jnp.bfloat16)] * 2,
        compiler_params=pltpu.CompilerParams(vmem_limit_bytes=56 * 2**20),
        cost_estimate=pl.CostEstimate(flops=2**20, bytes_accessed=2**12, transcendentals=0),
    )(rows, down, ups, factor)


def token_sums_kernel(near, out):
    total = None
    for e in range(4):
        wide = near[e].astype(jnp.float32)
        part = jnp.sum(wide * wide, axis=1, keepdims=True)
        total = part if total is None else total + part
    out[...] = total


def token_sums(near):
    return pl.pallas_call(
        token_sums_kernel,
        out_shape=jax.ShapeDtypeStruct((512, 1), jnp.float32),
        compiler_params=pltpu.CompilerParams(vmem_limit_bytes=56 * 2**20),
        cost_estimate=pl.CostEstimate(flops=2**20, bytes_accessed=2**12, transcendentals=0),
    )(near)


def multiply_slabs_kernel(place, *refs):
    count = (place.shape[0] - 2) // 2
    slabs, refs = refs[: 3 * count], refs[3 * count :]
    inverse, ups, factor = refs[:3]
    blocks, rest = refs[3 : 3 + 2 * count], refs[3 + 2 * count :]
    value = None
    for i in range(count):
        near, far, gain = slabs[3 * i : 3 * i + 3]
        block_a, block_b = blocks[2 * i : 2 * i + 2]
        for half in range(2):
            tokens = jnp.where(place[2 * count] == half, near[0], far[0]).astype(jnp.float32)
            normed = (tokens * inverse[...] * gain[0, half]).astype(jnp.bfloat16)
            merged = jnp.dot(block_a[0], ups[half], preferred_element_type=jnp.float32)
            tiles = []
            for k in range(5):
                rows = block_a[1 + k] if half == 0 else block_b[k]
                tiles.append(merged[:, k * 128 : (k + 1) * 128] + rows.astype(jnp.float32))
            weight = (jnp.concatenate(tiles, axis=1) * factor[...]).astype(jnp.bfloat16)
            part = jnp.dot(normed, weight, preferred_element_type=jnp.float32)
            value = part if value is None else value + part
    if len(rest) == 1:
        rest[0][...] = value
    else:
        value = value + rest[0][...]
        swapped = place[2 * count + 1] == 1
        rest[1][:256] = jnp.where(swapped, value[256:], value[:256])
        rest[1][256:] = jnp.where(swapped, value[:256], value[256:])


def multiply_slabs(place, near, far, inverse, gains, blocks, ups, factor, total):
    count = len(blocks) // 2

    def whole(shape):
        return pl.BlockSpec(shape, lambda i, place: (0,) * len(shape))

    operands, specs = [], []
    for k in range(count):
        operands += [near, far, gains]
        specs += [pl.BlockSpec((1, 512, 512), lambda i, place, k=k: (place[k], 0, 0))] * 2
        specs.append(
            pl.BlockSpec((1, 2, 1, 512), lambda i, place, k=k: (place[count + k], 0, 0, 0))
        )
    rest = [inverse, ups, factor, *blocks] + ([] if total is None else [total])
    operands += rest
    specs += [whole(operand.shape) for operand in rest]
    return pl.pallas_call(
        multiply_slabs_kernel,
        grid_spec=pltpu.PrefetchScalarGridSpec(
            num_scalar_prefetch=1,
            grid=(1,),
            in_specs=specs,
            out_specs=whole((512, 640)),
        ),
        out_shape=jax.ShapeDtypeStruct((512, 640), jnp.float32),
        compiler_params=pltpu.CompilerParams(vmem_limit_bytes=56 * 2**20),
        cost_estimate=pl.CostEstimate(
            flops=2**20, bytes_accessed=2**12, transcendentals=0
        ),
    )(place, *operands)


def attend_kernel(place, lengths, every, keys, values, out):
    f32, bf16 = jnp.float32, jnp.bfloat16
    inv_root = 1.0 / math.sqrt(128)
    both = every[...].astype(f32)
    fresh_keys = every[0, :, 512:]
    fresh_values = every[1, :, 512:]
    contract_last = (((1,), (1,)), ((), ()))
    fresh_column = lax.broadcasted_iota(jnp.int32, (128, 16), 1)
    fresh_row = lax.broadcasted_iota(jnp.int32, (128, 16), 0)
    slots = lax.broadcasted_iota(jnp.int32, (32, 1024), 1)
    blank = jnp.zeros((32, 128), bf16)
    queries = [
        jnp.concatenate(
            [
                both[h // 4, b * 4 : b * 4 + 4, (h % 4) * 128 : (h % 4 + 1) * 128]
                for h in range(8)
            ],
            axis=0,
        ).astype(bf16)
        for b in range(4)
    ]
    fresh = lax.dot_general(
        jnp.concatenate(queries, axis=0), fresh_keys, contract_last, preferred_element_type=f32
    )
    own = (fresh_row // 32) * 4
    order = (fresh_column >= own) & (fresh_column - own <= fresh_row % 4)
    fresh = jnp.where(order, fresh * inv_root, NEG_LARGE)
    scores = []
    for b in (0, 2):
        query = jnp.concatenate(
            [
                jnp.concatenate([queries[b], blank], axis=1),
                jnp.concatenate([blank, queries[b + 1]], axis=1),
            ],
            axis=0,
        )
        key = jnp.concatenate([keys[b, 0], keys[b + 1, 0]], axis=1)
        scores.append(
            lax.dot_general(query, key, contract_last, preferred_element_type=f32)
        )
    live = jnp.concatenate([slots < lengths[b] for b in range(4)], axis=0)
    scores = jnp.where(live, jnp.concatenate(scores, axis=0) * inv_root, NEG_LARGE)
    peak = jnp.maximum(
        jnp.max(scores, axis=1, keepdims=True), jnp.max(fresh, axis=1, keepdims=True)
    )
    probs = jnp.where(live, jnp.exp(scores - peak), 0.0)
    fresh_probs = jnp.where(order, jnp.exp(fresh - peak), 0.0)
    total = jnp.sum(probs, axis=1, keepdims=True) + jnp.sum(fresh_probs, axis=1, keepdims=True)
    rounded = probs.astype(bf16)
    contexts = []
    for b in (0, 2):
        value = jnp.concatenate([values[b, 0], values[b + 1, 0]], axis=1)
        part = jnp.dot(rounded[b * 32 : b * 32 + 64], value, preferred_element_type=f32)
        contexts += [part[:32, :128], part[32:, 128:]]
    context = jnp.concatenate(contexts, axis=0)
    context += jnp.dot(fresh_probs.astype(bf16), fresh_values, preferred_element_type=f32)
    context = context / total
    pieces = [
        jnp.concatenate(
            [context[b * 32 + h * 4 : b * 32 + h * 4 + 4] for h in range(8)], axis=1
        )
        for b in range(4)
    ]
    out[0] = jnp.concatenate(pieces, axis=0).astype(bf16)


def attend(place, lengths, every, cached_key_rows, cached_value_rows):
    def slab(g, place, lengths):
        return (((g + place[1]) % 2) * 4 + (g // 2 + 4 - place[0]) % 4, 0, 0)

    cache = pl.BlockSpec((4, 1, 1024, 128), lambda g, place, lengths: (0, g, 0, 0))
    return pl.pallas_call(
        attend_kernel,
        grid_spec=pltpu.PrefetchScalarGridSpec(
            num_scalar_prefetch=2,
            grid=(8,),
            in_specs=[
                pl.BlockSpec((2, 16, 640), lambda g, place, lengths: (g, 0, 0)),
                cache,
                cache,
            ],
            out_specs=pl.BlockSpec((1, 16, 1024), slab),
        ),
        out_shape=jax.ShapeDtypeStruct((8, 16, 1024), jnp.bfloat16),
        compiler_params=pltpu.CompilerParams(vmem_limit_bytes=56 * 2**20),
        cost_estimate=pl.CostEstimate(flops=2**20, bytes_accessed=2**12, transcendentals=0),
    )(place, lengths, every, cached_key_rows, cached_value_rows)


def output_kernel(place, near_a, near_b, far_a, far_b, *refs):
    weights, (mine, other) = refs[:8], refs[8:]
    total = None
    for j in range(4):
        parts = []
        for first, second in ((near_a, near_b), (far_a, far_b)):
            if j < 2:
                parts.append(first[:, :, j].reshape(256, 1024))
            else:
                parts.extend(second[:, e, j - 2].reshape(64, 1024) for e in range(4))
        rows = jnp.concatenate(parts, axis=0)
        for half in range(2):
            part = jnp.dot(
                rows[:, half * 512 : (half + 1) * 512],
                weights[2 * j + half][...],
                preferred_element_type=jnp.float32,
            )
            total = part if total is None else total + part
    for cr in range(2):
        for e in range(4):
            for dl in range(2):
                for dh in range(2):
                    start = cr * 256 + e * 64 + dl * 32 + dh * 16
                    target = ((place[0] + e) % 4) * 4 + (place[1] ^ dh) * 2 + (place[2] ^ cr)
                    rows = total[start : start + 16]
                    if dl == 0:
                        mine[target] = rows
                    else:
                        other[target] = rows.astype(jnp.bfloat16)


def multiply_output(place, pieces, rows_o):
    def whole(shape):
        return pl.BlockSpec(shape, lambda i, place: (0,) * len(shape))

    operands = [*pieces, *rows_o]
    return pl.pallas_call(
        output_kernel,
        grid_spec=pltpu.PrefetchScalarGridSpec(
            num_scalar_prefetch=1,
            grid=(1,),
            in_specs=[whole(operand.shape) for operand in operands],
            out_specs=[whole((16, 16, 512)), whole((16, 16, 512))],
        ),
        out_shape=[
            jax.ShapeDtypeStruct((16, 16, 512), jnp.float32),
            jax.ShapeDtypeStruct((16, 16, 512), jnp.bfloat16),
        ],
        compiler_params=pltpu.CompilerParams(vmem_limit_bytes=40 * 2**20),
        cost_estimate=pl.CostEstimate(flops=2**31, bytes_accessed=2**23, transcendentals=0),
    )(place, *operands)


def per_device(
    token_hidden_rows,
    input_norm_gain,
    frozen_query,
    frozen_key_value,
    frozen_output,
    query_down_factor,
    query_up_factor,
    key_value_down_factor,
    key_value_up_factor,
    output_down_factor,
    output_up_factor,
    query_column_scale,
    key_value_column_scale,
    output_column_scale,
    cached_key_rows,
    cached_value_rows,
    lengths,
):
    f32, bf16 = jnp.float32, jnp.bfloat16
    r, t = lax.axis_index("rep"), lax.axis_index("tp")
    y, zl = r // 2, r % 2
    x, zh, c = t // 4, (t // 2) % 2, t % 2

    local = token_hidden_rows.transpose(1, 0, 2).reshape(256, 512)
    pair = jnp.concatenate(
        [
            permute(local, lambda y, zl, x, zh, c, s=s: (y, zh, x, zl ^ s, c))
            for s in range(2)
        ]
    )

    frozen = pack_columns(
        t.astype(jnp.int32).reshape(1),
        frozen_query,
        frozen_key_value,
        frozen_output,
        query_down_factor.T,
        key_value_down_factor.T,
        output_down_factor.T,
    )
    received = lax.all_to_all(frozen, "tp", 0, 0, tiled=True)

    up_q = lax.dynamic_slice_in_dim(query_up_factor, t * 512, 512, 1)
    up_kv = lax.dynamic_slice_in_dim(key_value_up_factor, t * 128, 128, 1)
    up_o = lax.dynamic_slice_in_dim(output_up_factor, t * 512, 512, 1)
    up_qkv = jnp.concatenate(
        [
            jnp.concatenate([up_q, jnp.zeros((32, 128), bf16)], axis=1),
            jnp.concatenate([jnp.zeros((32, 512), bf16), up_kv], axis=1),
        ],
        axis=0,
    )
    blank = jnp.zeros((64, 640), bf16)
    ups = jnp.stack(
        [jnp.concatenate([up_qkv, blank], axis=0), jnp.concatenate([blank, up_qkv], axis=0)]
    )
    blank = jnp.zeros((32, 512), bf16)
    ups_out = jnp.stack(
        [
            jnp.concatenate([blank, blank, up_o, blank]),
            jnp.concatenate([up_o, blank, blank, blank]),
        ]
    )
    scale_qkv = jnp.concatenate(
        [
            lax.dynamic_slice_in_dim(query_column_scale, t * 512, 512, 0),
            lax.dynamic_slice_in_dim(key_value_column_scale, t * 128, 128, 0),
        ]
    )
    scale_out = lax.dynamic_slice_in_dim(output_column_scale, t * 512, 512, 0)

    received, ups, ups_out, scale_qkv, scale_out = lax.optimization_barrier(
        (received, ups, ups_out, scale_qkv, scale_out)
    )
    own_a, own_b, own_o, down_own, sums = unpack_columns(received, ups, ups_out)

    sums = sums.reshape(1152)
    sums = [sums] + [from_y(sums, step) for step in (1, 2, 3)]
    own_a, own_b, pair, sums = lax.optimization_barrier((own_a, own_b, pair, sums))

    next_a, last_b = from_y(own_a, 1), from_y(own_b, 3)
    next_b, last_a = from_y(own_b, 1), from_y(own_a, 3)
    tokens = [pair] + [from_x(pair, step) for step in (1, 2, 3)]
    near = jnp.stack(tokens)
    sums = sum(sums)
    sums = sums + swap_low(sums)
    factor_qkv = (scale_qkv / jnp.sqrt(sums[:640])).reshape(1, 640)
    factor_out = (scale_out / jnp.sqrt(sums[640:])).reshape(1, 512)
    weight_a, weight_b = scale_rows(own_o, down_own, ups_out, factor_out)
    next_a, next_b, last_a, last_b, near, factor_qkv, weight_a, weight_b = (
        lax.optimization_barrier(
            (next_a, next_b, last_a, last_b, near, factor_qkv, weight_a, weight_b)
        )
    )
    far_a, far_b = from_y(next_a, 1), from_y(last_b, 3)
    far = swap_core(near)
    squares = token_sums(near).reshape(512)
    squares = squares + swap_core(squares)
    squares = squares + swap_low(squares)
    inverse = lax.rsqrt(squares / 8192.0 + EPSILON).reshape(512, 1)

    gains = pick(input_norm_gain.reshape(4, 2, 2, 1, 512), zl, 1)

    def project(steps, blocks, total):
        place = [(y + step - x) % 4 for step in steps] + [(y + step) % 4 for step in steps]
        place = jnp.stack(place + [c, zh]).astype(jnp.int32)
        return multiply_slabs(
            place, near, far, inverse, gains, blocks, ups, factor_qkv, total
        )

    total = project((0, 1, 3), (own_a, own_b, next_a, next_b, last_a, last_b), None)
    total, far_a, far_b = lax.optimization_barrier((total, far_a, far_b))
    total = project((2,), (far_a, far_b), total)

    first_rows, last_rows = from_y(weight_a, 1), from_y(weight_b, 3)
    total, first_rows, last_rows = lax.optimization_barrier((total, first_rows, last_rows))
    rows_o = [weight_a, weight_b, first_rows, from_y(weight_b, 1)]
    rows_o += [from_y(first_rows, 1), from_y(last_rows, 3), from_y(weight_a, 3), last_rows]

    groups = [[32 * k + i for i in range(32)] for k in range(4)]
    halves = lax.all_to_all(
        total.reshape(32, 16, 640), AXES, 0, 0, axis_index_groups=groups, tiled=True
    )
    every = jnp.sum(halves.reshape(2, 16, 16, 640), axis=0).astype(bf16)

    place = jnp.stack([y, zl]).astype(jnp.int32)
    attended = attend(place, lengths, every, cached_key_rows, cached_value_rows)

    attended, rows_o = lax.optimization_barrier((attended, rows_o))
    slabs = attended.reshape(2, 4, 16, 1024)

    def along_z(own, other):
        def flip(value, dl, dh):
            return permute(value, lambda y, zl, x, zh, c: (y, zl ^ dl, x, zh ^ dh, c))

        return jnp.stack([own, flip(own, 0, 1), flip(other, 1, 0), flip(other, 1, 1)])

    def along_x(value):
        return jnp.stack([value] + [from_x(value, step) for step in (1, 2, 3)])

    first = jnp.stack([slabs[0, :2], swap_low(slabs[1, :2])])
    flipped = permute(first, lambda y, zl, x, zh, c: (y, zl, x, 1 - zh, c))
    first = jnp.stack([first[0], flipped[0], first[1], flipped[1]])
    second = along_x(slabs[:, 2:])
    first = along_x(first)
    second = along_z(second[:, 0], second[:, 1])
    place = jnp.stack([x, zh, c]).astype(jnp.int32)
    mine, other = multiply_output(
        place, (first, second, swap_core(first), swap_core(second)), rows_o
    )
    result = (mine + swap_low(other).astype(f32)).astype(bf16)
    return result.reshape(16, 4, 4, 512).transpose(2, 0, 1, 3).reshape(4, 64, 512)


def solution(mesh):
    return jax.shard_map(
        per_device,
        mesh=mesh,
        in_specs=(
            P(None, "rep", "tp"),
            P(),
            P(("rep", "tp"), None),
            P(("rep", "tp"), None),
            P(("rep", "tp"), None),
            P(("rep", "tp"), None),
            P(),
            P(("rep", "tp"), None),
            P(),
            P(("rep", "tp"), None),
            P(),
            P(),
            P(),
            P(),
            P(("rep", "tp"), None, None, None),
            P(("rep", "tp"), None, None, None),
            P(("rep", "tp")),
        ),
        out_specs=P(None, "rep", "tp"),
        check_vma=False,
    )
```
